32 devices in a mesh: dp: 8 (over z, y), expert: 4 (over x, core).
Axes of the slice: x: 2, y: 2, z: 4, core: 2. Of those that a mesh axis runs over, the one named last changes fastest.
Arguments:
- hidden: bfloat16 [4, 1024, 8192], P('expert', None, 'dp'), may hold values from -6 to 6
- down_weight: bfloat16 [4, 8192, 6144], P('expert', 'dp'), may hold values from -0.0625 to 0.0625
- grad_out: bfloat16 [1024, 6144], P('dp', 'expert'), may hold values from -2 to 2
- routing: int32 [1024, 2], P('dp'), may hold values from 0 to 3, all different within a row; in each aligned block of 128 rows (0 to 127, 128 to 255, ...) at most 128 rows name the same one
- gates: float32 [1024, 2], P('dp'), may hold values from 0.25 to 1
Outputs:
- mixed_out: bfloat16 [1024, 6144], P('dp', 'expert')
- grad_hidden: bfloat16 [4, 1024, 8192], P('expert', None, 'dp')
- grad_weight: bfloat16 [4, 8192, 6144], P('expert', 'dp')
The draws below stay inside these ranges and needn't reach their ends.
Inputs may be any that keep to these rules, and one draw needn't show every extreme that they name: `routing`: among the 128 tokens of one sequence shard (aligned blocks of rows), each expert is named by at most 128 tokens, a bound that some block reaches; a token names 2 different experts.
All inputs are finite; a program needn't handle non-finite values.
Results may differ from the reference program's by a relative error of at most 0.017.
Values may be sent and summed in bfloat16 or wider, within the bound.
No kernel may reach another device: no remote copies, remote signals or barrier semaphores. Data moves between devices by JAX's collectives and lax.ppermute only.
A program may use at most 128 MiB of HBM per device.

```python
import math
import jax
import jax.numpy as jnp
import numpy as np
from jax import lax

D = 6144
TOP = 2
HID = 8192
TOK_DEV = 128
EXPERTS = 4
CAP = 128
SLOTS = 1024
TOKENS = 1024
N_DP = 8


def with_spikes(array, rng, source, target, blocks, factor):
    owner, partner = [(jnp.arange(array.shape[axis_at]) // (array.shape[axis_at] // blocks)).reshape([-1 if axis == axis_at else 1 for axis in range(array.ndim)]) for axis_at in (source, target)]
    chosen = jax.random.permutation(rng, blocks)[partner]
    strong = (owner == chosen) | (owner == (partner + blocks // 2) % blocks)
    return jnp.where(strong, factor * array, array)


def steps_of(rng, shape, split, least, largest):
    loudness, own = 1.0, jax.random.fold_in(rng, 6)
    for dim, blocks in split:
        draws = jnp.exp(jax.random.uniform(jax.random.fold_in(own, dim), (blocks,), jnp.float32, least / len(split), largest / len(split)))
        loudness = loudness * jnp.repeat(draws, shape[dim] // blocks).reshape([-1 if axis == dim else 1 for axis in range(len(shape))])
    return loudness


def shared_out(own_key, own, number, rows, number_of, top, reach, lean):
    order = jax.random.permutation(own_key, number_of)
    crowded, common = shares(number_of, rows * top, reach, lean, True), shares(number_of, rows * top, reach, lean, False)
    places = jnp.arange(number_of)

    def named(sizes, offset_by):
        used = int((sizes > 0).sum())
        fixed = max(1, used // 4)
        shifted = fixed + (places - fixed + offset_by * (used - fixed)) % max(1, number_of - fixed)
        return jnp.zeros((number_of,), jnp.int32).at[order[jnp.where(places < fixed, places, shifted)]].set(jnp.asarray(sizes, jnp.int32))

    sizes = jnp.where(number % 4 == 0, named(crowded, number // 4), named(common, number - number // 4 - 1))
    mixed = jax.random.permutation(jax.random.fold_in(own, 3), number_of)
    giver, sink = mixed[0:number_of // 2 * 2:2], mixed[1:number_of // 2 * 2:2]
    room = jnp.minimum(sizes[giver] - 1, reach - sizes[sink]) // 2
    room = jnp.where((giver == order[0]) | (sink == order[0]) | (sizes[sink] == 0), 0, jnp.maximum(room, 0))
    shifted = jax.random.randint(jax.random.fold_in(own, 4), (number_of // 2,), 0, 1 << 20) % (room + 1)
    sizes = sizes.at[giver].add(-shifted).at[sink].add(shifted)
    members = jnp.searchsorted(jnp.cumsum(sizes), jnp.arange(rows * top), side="right").astype(jnp.int32)
    table = members.reshape(top, rows).T
    table = table[jax.random.permutation(jax.random.fold_in(own, 1), rows)]
    offset_by = jax.random.randint(jax.random.fold_in(own, 2), (rows, 1), 0, top)
    return jnp.take_along_axis(table, (jnp.arange(top)[None, :] + offset_by) % top, axis=1)


def shares(amount, total, limit, skew, full):
    weights = [(1 << 20) // math.isqrt(grade ** skew) + 1 for grade in range(1, amount + 1)]
    largest = limit if full else min(limit, max(-(-total // amount), total * weights[0] // sum(weights)))
    least = 1 if total - largest >= amount - 1 else 0
    counts, spare = [largest] + [least] * (amount - 1), total - largest - least * (amount - 1)
    while spare > 0:
        free = [i for i in range(1, amount) if counts[i] < largest] or [i for i in range(1, amount) if counts[i] < limit]
        pool, budget = sum([weights[i] for i in free]), spare
        for i in free:
            addition = min(limit - counts[i], max(1, budget * weights[i] // pool), spare)
            counts[i] = counts[i] + addition
            spare = spare - addition
    return np.array(counts)


def scatter_about(stream_key, shape, deviation, limit, cuts=(), kind=jnp.bfloat16):
    result = deviation * jax.random.normal(stream_key, shape, jnp.float32)
    if cuts:
        result = result * steps_of(stream_key, shape, cuts, -0.22, 0.18)
    return jnp.clip(result, -limit, limit).astype(kind)


def bell_draw_with(rng, extent, deviation, most, cuts, heavy, kind=jnp.bfloat16):
    array = deviation * jax.random.normal(rng, extent, jnp.float32)
    if cuts:
        array = array * steps_of(rng, extent, cuts, -0.22, 0.18)
    return jnp.clip(with_spikes(array, jax.random.fold_in(rng, 3), *heavy), -most, most).astype(kind)


def setup_inputs(seed: int = 0) -> dict:
    splits = jax.random.split(jax.random.key(seed), 6)
    hidden = bell_draw_with(splits[0], (EXPERTS, SLOTS, HID), 1.0, 6.0, ((0, 4), (2, 8)), (2, 1, 8, 2.0))
    down_weight = scatter_about(splits[1], (EXPERTS, HID, D), HID ** -0.5, 0.0625, ((0, 4), (1, 8)))
    grad_out = scatter_about(splits[2], (TOKENS, D), 0.3, 2.0, ((0, 8), (1, 4)))
    routing_keys = jax.random.split(jax.random.fold_in(splits[3], 1), TOKENS // TOK_DEV)
    routing_turns = jax.random.permutation(jax.random.fold_in(splits[3], 3), TOKENS // TOK_DEV)
    routing = jax.vmap(lambda own, number: shared_out(jax.random.fold_in(splits[3], 2), own, number, TOK_DEV, EXPERTS, TOP, CAP, 2))(routing_keys, routing_turns).reshape((TOKENS, TOP))
    gates = jnp.clip(0.25 + 0.75 * jax.random.uniform(splits[4], (TOKENS, TOP), jnp.float32) ** steps_of(splits[4], (TOKENS, TOP), ((0, 8),), -0.2, 0.2), 0.25, 1.0)
    return dict(hidden=hidden, down_weight=down_weight, grad_out=grad_out, routing=routing, gates=gates)


def dispatch_weights(routing, gates, experts, capacity):
    flattened = routing.reshape(-1).astype(jnp.int32)
    onehot = (flattened[:, None] == jnp.arange(experts, dtype=jnp.int32)[None, :]).astype(jnp.int32)
    position = jnp.sum((jnp.cumsum(onehot, axis=0) - onehot) * onehot, axis=1)
    target = flattened * capacity + position
    picked = (jnp.arange(experts * capacity, dtype=jnp.int32)[:, None] == target[None, :]).astype(jnp.float32)
    picked = picked * gates.reshape(-1)[None, :].astype(jnp.float32)
    return jnp.sum(picked.reshape(experts * capacity, routing.shape[0], routing.shape[1]), axis=2)


def shard_dispatch(shard_routes, shard_gates):
    return dispatch_weights(shard_routes, shard_gates, EXPERTS, CAP)


def reference(hidden, down_weight, grad_out, routing, gates):
    highest = lax.Precision.HIGHEST
    width = HID // N_DP
    dispatch = jax.vmap(shard_dispatch)(routing.reshape(N_DP, TOK_DEV, TOP), gates.reshape(N_DP, TOK_DEV, TOP))
    expert_outs = []
    for expert_id in range(EXPERTS):
        total = jnp.zeros((SLOTS, D), jnp.float32)
        for block_id in range(N_DP):
            lower = block_id * width
            part = jnp.dot(hidden[expert_id, :, lower:lower + width], down_weight[expert_id, lower:lower + width, :], preferred_element_type=jnp.float32)
            rounded = lax.optimization_barrier(part.astype(jnp.bfloat16))
            total = total + rounded.astype(jnp.float32)
        expert_outs.append(total.astype(jnp.bfloat16))
    stacked = jnp.stack(expert_outs).reshape(EXPERTS, N_DP, CAP, D).transpose(1, 0, 2, 3)
    stacked = stacked.reshape(N_DP, EXPERTS * CAP, D).astype(jnp.float32)
    mixed_out = jnp.einsum("dst,dsf->dtf", dispatch, stacked, precision=highest)
    mixed_out = mixed_out.reshape(TOKENS, D).astype(jnp.bfloat16)
    grads = grad_out.reshape(N_DP, TOK_DEV, D).astype(jnp.float32)
    routed = jnp.einsum("dst,dtf->dsf", dispatch, grads, precision=highest).astype(jnp.bfloat16)
    routed = routed.reshape(N_DP, EXPERTS, CAP, D).transpose(1, 0, 2, 3).reshape(EXPERTS, SLOTS, D)
    grad_hidden = []
    grad_weight = []
    for expert_id in range(EXPERTS):
        grad_hidden.append(jnp.dot(routed[expert_id], down_weight[expert_id].T, preferred_element_type=jnp.float32).astype(jnp.bfloat16))
        grad_weight.append(jnp.dot(hidden[expert_id].T, routed[expert_id], preferred_element_type=jnp.float32).astype(jnp.bfloat16))
    return (mixed_out, jnp.stack(grad_hidden), jnp.stack(grad_weight))
```

```python
import functools
import jax
import jax.numpy as jnp
from jax import lax
from jax.experimental import pallas as pl
from jax.experimental.pallas import tpu as pltpu
from jax.sharding import PartitionSpec as P

BF16, F32 = jnp.bfloat16, jnp.float32


class Ring:
    def __init__(self, name, total, size, inner):
        self.name, self.size = name, size
        self.perm = []
        for i in range(total):
            here = (i // inner) % size
            self.perm.append((i, i + (((here + 1) % size) - here) * inner))
        self.place = (lax.axis_index(name) // inner) % size

    def shift(self, block):
        return lax.ppermute(block, self.name, self.perm)

    def gather(self, block):
        blocks = [block]
        for _ in range(self.size - 1):
            blocks.append(self.shift(blocks[-1]))
        return blocks

    def scatter(self, blocks):
        if self.size == 1:
            return blocks[0]
        total = blocks[1]
        for j in list(range(2, self.size)) + [0]:
            total = blocks[j] + self.shift(total)
        return total


def tile_of(width, most=512):
    tile = most
    while width % tile:
        tile -= 128
    return tile


def forward_kernel(quarter, rows, weight, *rest):
    out = rest[-1]
    acc = jnp.dot(rows[...], weight[...], preferred_element_type=F32)
    if len(rest) == 2:
        acc = acc + rest[0][0].astype(F32)
    out[0] = acc.astype(BF16)


def forward(rows, weight, quarters, extra=None):
    count = quarters.shape[0]
    tokens, depth = rows.shape
    width = weight.shape[1] // (lax.axis_size("expert"))
    tile = tile_of(width)
    per = width // tile
    specs = [
        pl.BlockSpec((tokens, depth), lambda i, j, q: (0, 0)),
        pl.BlockSpec((depth, tile), lambda i, j, q: (0, q[i] * per + j)),
    ]
    operands = [rows, weight]
    block = pl.BlockSpec((1, tokens, tile), lambda i, j, q: (i, 0, j))
    if extra is not None:
        specs.append(block)
        operands.append(extra)
    return pl.pallas_call(
        forward_kernel,
        grid_spec=pltpu.PrefetchScalarGridSpec(
            num_scalar_prefetch=1, grid=(count, per), in_specs=specs, out_specs=block
        ),
        out_shape=jax.ShapeDtypeStruct((count, tokens, width), BF16),
        compiler_params=pltpu.CompilerParams(vmem_limit_bytes=40 * 2**20),
        cost_estimate=pl.CostEstimate(
            flops=2 * tokens * depth * width * count,
            bytes_accessed=2 * (tokens * depth + count * width * (depth + tokens)),
            transcendentals=0,
        ),
        name="forward_rows",
    )(quarters, *operands)


def backward_kernel(steps, first, last, quarter, rows, grads, weight, *rest):
    rest = list(rest)
    gates = rest.pop(0) if last else None
    if not first:
        before, _ = rest.pop(0), rest.pop(0)
    weight_out, hidden_out, turned, total = rest
    step = pl.program_id(0) * pl.num_programs(1) + pl.program_id(1)

    @pl.when(step == 0)
    def _():
        turned[...] = rows[...].T
        total[...] = jnp.zeros_like(total) if first else before[...]

    block = grads[0]
    weight_out[...] = jnp.dot(turned[...], block, preferred_element_type=F32).astype(BF16)
    total[...] += lax.dot_general(
        block, weight[...], (((1,), (1,)), ((), ())), preferred_element_type=F32
    )

    @pl.when(step == steps - 1)
    def _():
        if last:
            hidden_out[...] = (total[...] * gates[...]).astype(BF16)
        else:
            hidden_out[...] = total[...]


def backward(rows, grads, weight, quarters, gates, before):
    count, tokens, width = grads.shape
    depth = rows.shape[1]
    tile = tile_of(width)
    per = width // tile
    first, last = before is None, gates is not None
    whole = lambda shape: pl.BlockSpec(shape, lambda i, j, q: (0, 0))
    specs = [
        whole((tokens, depth)),
        pl.BlockSpec((1, tokens, tile), lambda i, j, q: (i, 0, j)),
        pl.BlockSpec((depth, tile), lambda i, j, q: (0, q[i] * per + j)),
    ]
    operands = [rows, grads, weight]
    aliases = {}
    if last:
        specs.append(whole((tokens, 1)))
        operands.append(gates)
    if not first:
        specs += [whole((tokens, depth)), pl.BlockSpec(memory_space=pl.ANY)]
        operands += [before[1], before[0]]
        aliases = {len(operands): 0}
    return pl.pallas_call(
        functools.partial(backward_kernel, count * per, first, last),
        grid_spec=pltpu.PrefetchScalarGridSpec(
            num_scalar_prefetch=1,
            grid=(count, per),
            in_specs=specs,
            out_specs=[
                pl.BlockSpec((depth, tile), lambda i, j, q: (0, q[i] * per + j)),
                whole((tokens, depth)),
            ],
            scratch_shapes=[pltpu.VMEM((depth, tokens), BF16), pltpu.VMEM((tokens, depth), F32)],
        ),
        out_shape=[
            jax.ShapeDtypeStruct(weight.shape, BF16),
            jax.ShapeDtypeStruct((tokens, depth), BF16 if last else F32),
        ],
        input_output_aliases=aliases,
        compiler_params=pltpu.CompilerParams(vmem_limit_bytes=48 * 2**20),
        cost_estimate=pl.CostEstimate(
            flops=4 * tokens * depth * width * count,
            bytes_accessed=2 * (2 * tokens * depth + count * width * (2 * depth + tokens)),
            transcendentals=0,
        ),
        name="backward_rows",
    )(quarters, *operands)


def routes(routing, gates, experts):
    flattened = routing.reshape(-1)
    onehot = (flattened[:, None] == jnp.arange(experts, dtype=jnp.int32)[None, :]).astype(jnp.int32)
    before = jnp.cumsum(onehot, axis=0) - onehot
    slot = jnp.where(onehot > 0, before + 1, 0).reshape(routing.shape + (experts,)).sum(axis=1) - 1
    gate = (onehot.reshape(routing.shape + (experts,)) * gates[:, :, None]).sum(axis=1)
    return jnp.stack([slot.astype(F32).T, gate.T])


def body(hidden, down_weight, grad_out, routing, gates):
    groups, owners = lax.axis_size("dp"), lax.axis_size("expert")
    cores = 2 if owners % 2 == 0 else 1
    nx = owners // cores
    ny = nx if groups % nx == 0 else 1
    nz = groups // ny
    ring_c = Ring("expert", owners, cores, 1)
    ring_x = Ring("expert", owners, nx, cores)
    ring_y = Ring("dp", groups, ny, 1)
    ring_z = Ring("dp", groups, nz, ny)
    rows, width = grad_out.shape
    slots = hidden.shape[1]
    capacity = slots // groups
    experts = hidden.shape[0] * owners
    hidden_rows, weight = hidden[0], down_weight[0]
    third = rows // 4
    pair = (rows - third) // 2
    parts = {"a": (0, pair), "b": (pair, 2 * pair), "c": (2 * pair, rows)}

    late = list(range(1, nz)) + [0]
    turns = [late[: nz // 2], late[nz // 2 :]] if nz > 1 else [late]
    order = []
    starts = {}
    at = 0
    for part in "ab":
        for turn_at, turn in enumerate(turns):
            starts[part, turn_at] = at
            for jy in range(ny):
                for jz in turn:
                    order.append((part, jz, jy))
                    at += pair
    starts["c"] = at
    for jz in range(nz):
        for jy in range(ny):
            order.append(("c", jz, jy))

    have = {}
    c_x = jnp.stack(ring_x.gather(grad_out[2 * pair :]))
    c_y = jnp.stack(ring_y.gather(c_x))
    c_z = ring_z.gather(c_y)
    for jz in range(nz):
        for jy in range(ny):
            have["c", jz, jy] = [c_z[jz][jy, jx] for jx in range(nx)]
    ab = ring_z.gather(grad_out[: 2 * pair])
    early = list(range(nz))
    for turn in [early[: nz // 2], early[nz // 2 :]] if nz > 1 else [early]:
        a = jnp.stack([ab[jz][:pair] for jz in turn])
        b = jnp.stack([ab[jz][pair:] for jz in turn])
        a_xy = ring_x.gather(jnp.stack(ring_y.gather(a)))
        b_yx = ring_y.gather(jnp.stack(ring_x.gather(b)))
        for i, jz in enumerate(turn):
            for jy in range(ny):
                have["a", jz, jy] = [a_xy[jx][jy, i] for jx in range(nx)]
                have["b", jz, jy] = [b_yx[jy][jx, i] for jx in range(nx)]
    grads = jnp.stack([jnp.concatenate([have[key][jx] for key in order]) for jx in range(nx)])

    expert = lax.axis_index("expert")
    table = lax.all_gather(routes(routing, gates, experts), "dp")
    table = lax.dynamic_index_in_dim(table, expert, axis=2, keepdims=False)
    shard = jnp.arange(groups, dtype=F32)[:, None]
    slot = jnp.where(table[:, 0] >= 0, table[:, 0] + shard * capacity, -1.0)
    table = jnp.stack([slot, table[:, 1]])
    table = table.reshape(2, nz, ny, rows)
    back_z = (ring_z.place - jnp.arange(nz)) % nz
    back_y = (ring_y.place - jnp.arange(ny)) % ny
    table = table[:, back_z][:, :, back_y]
    table = jnp.concatenate(
        [table[:, jz, jy, parts[part][0] : parts[part][1]] for part, jz, jy in order], axis=1
    )
    slot_of, gate_of = table[0].astype(jnp.int32), table[1]
    chosen = slot_of[:, None] == jnp.arange(slots, dtype=jnp.int32)[None, :]
    chosen = chosen.astype(BF16)
    gate_column = gate_of[:, None]
    rows_in = jnp.dot(chosen, hidden_rows, preferred_element_type=F32)
    rows_in = (rows_in * gate_column).astype(BF16)

    back_x = (ring_x.place - jnp.arange(nx)) % nx * cores
    mine = (back_x + ring_c.place).astype(jnp.int32)
    theirs = [(back_x + (ring_c.place - jc) % cores).astype(jnp.int32) for jc in range(1, cores)]
    if cores > 1:
        partial = forward(rows_in, weight, theirs[0])
        partial = forward(rows_in, weight, mine, ring_c.shift(partial))
    else:
        partial = forward(rows_in, weight, mine)
    sums = {}
    for turn_at, turn in enumerate(turns):
        size = len(turn) * pair
        start = starts["a", turn_at]
        a = ring_x.scatter([partial[jx, start : start + ny * size] for jx in range(nx)])
        a = ring_y.scatter([a[jy * size : (jy + 1) * size] for jy in range(ny)])
        start = starts["b", turn_at]
        b = ring_y.scatter(
            [partial[:, start + jy * size : start + (jy + 1) * size] for jy in range(ny)]
        )
        b = ring_x.scatter([b[jx] for jx in range(nx)])
        for i, jz in enumerate(turn):
            span = slice(i * pair, (i + 1) * pair)
            sums[jz] = jnp.concatenate([a[span], b[span]])
    ab_sum = ring_z.scatter([sums[jz] for jz in range(nz)])
    size = ny * third
    start = starts["c"]
    c = ring_z.scatter([partial[:, start + jz * size : start + (jz + 1) * size] for jz in range(nz)])
    c = ring_y.scatter([c[:, jy * third : (jy + 1) * third] for jy in range(ny)])
    c = ring_x.scatter([c[jx] for jx in range(nx)])
    mixed_out = jnp.concatenate([ab_sum, c])

    if cores > 1:
        before = backward(rows_in, grads, weight, mine, None, None)
        grad_weight, back = backward(
            rows_in, ring_c.shift(grads), weight, theirs[0], gate_column, before
        )
    else:
        grad_weight, back = backward(rows_in, grads, weight, mine, gate_column, None)
    grad_hidden = lax.dot_general(
        chosen, back, (((0,), (0,)), ((), ())), preferred_element_type=F32
    ).astype(BF16)
    return (mixed_out, grad_hidden[None], grad_weight[None])


def solution(mesh):
    return jax.shard_map(
        body,
        mesh=mesh,
        in_specs=(
            P("expert", None, "dp"),
            P("expert", "dp", None),
            P("dp", "expert"),
            P("dp", None),
            P("dp", None),
        ),
        out_specs=(P("dp", "expert"), P("expert", None, "dp"), P("expert", "dp", None)),
        check_vma=False,
    )
```

```python
import functools
import jax
import jax.numpy as jnp
from jax import lax
from jax.experimental import pallas as pl
from jax.experimental.pallas import tpu as pltpu
from jax.sharding import PartitionSpec as P

BF16, F32 = jnp.bfloat16, jnp.float32
ALL = ("dp", "expert")
VMEM = 44 * 2**20


class Ring:
    def __init__(self, size, perm):
        self.size, self.perm = size, perm

    def shift(self, block):
        return lax.ppermute(block, ALL, self.perm)

    def gather(self, block):
        blocks = [block]
        for _ in range(self.size - 1):
            blocks.append(self.shift(blocks[-1]))
        return blocks

    def scatter(self, blocks):
        if self.size == 1:
            return blocks[0]
        total = blocks[1]
        for j in list(range(2, self.size)) + [0]:
            total = blocks[j] + self.shift(total)
        return total


class Layout:
    def __init__(self):
        self.groups, self.owners = lax.axis_size("dp"), lax.axis_size("expert")
        self.nc = 2 if self.owners % 2 == 0 else 1
        self.nx = self.owners // self.nc
        self.ny = self.nx if self.groups % self.nx == 0 else 1
        self.nz = self.groups // self.ny
        dp, expert = lax.axis_index("dp"), lax.axis_index("expert")
        self.z, self.y = dp // self.ny, dp % self.ny
        self.x, self.core = expert // self.nc, expert % self.nc
        self.mixed = self.nx == self.ny and self.nc == 2
        step = {
            "x": lambda z, y, x, c: (z, y, (x + 1) % self.nx, c),
            "y": lambda z, y, x, c: (z, (y + 1) % self.ny, x, c),
            "c": lambda z, y, x, c: (z, y, x, (c + 1) % self.nc),
        }
        swapped = lambda c: self.mixed and c == 1
        self.far_z = [
            self.ring(self.nz, lambda z, y, x, c, k=k: ((z + k) % self.nz, y, x, c))
            for k in range(self.nz)
        ]
        self.ring_y = self.ring(self.ny, step["y"])
        self.ring_c = self.ring(self.nc, step["c"])
        self.ring_1 = self.ring(
            self.ny, lambda z, y, x, c: step["x" if swapped(c) else "y"](z, y, x, c)
        )
        self.ring_2 = self.ring(
            self.nx, lambda z, y, x, c: step["y" if swapped(c) else "x"](z, y, x, c)
        )

    def ring(self, size, onward):
        flat = lambda z, y, x, c: ((z * self.ny + y) * self.nx + x) * self.nc + c
        perm = []
        for z in range(self.nz):
            for y in range(self.ny):
                for x in range(self.nx):
                    for c in range(self.nc):
                        perm.append((flat(z, y, x, c), flat(*onward(z, y, x, c))))
        return Ring(size, perm)


def tile_of(width, most):
    tile = most
    while width % tile:
        tile -= 128
    return tile


def send_kernel(quarter, rows, weight, out):
    out[...] = jnp.dot(rows[...], weight[...], preferred_element_type=F32).astype(BF16)


def forward_sent(rows, weight, quarter):
    tokens, depth = rows.shape
    width = weight.shape[1] // lax.axis_size("expert")
    tile = tile_of(width, 768)
    per = width // tile
    return pl.pallas_call(
        send_kernel,
        grid_spec=pltpu.PrefetchScalarGridSpec(
            num_scalar_prefetch=1,
            grid=(per,),
            in_specs=[
                pl.BlockSpec((tokens, depth), lambda j, q: (0, 0)),
                pl.BlockSpec((depth, tile), lambda j, q: (0, q[0] * per + j)),
            ],
            out_specs=pl.BlockSpec((tokens, tile), lambda j, q: (0, j)),
        ),
        out_shape=jax.ShapeDtypeStruct((tokens, width), BF16),
        compiler_params=pltpu.CompilerParams(vmem_limit_bytes=VMEM),
        cost_estimate=pl.CostEstimate(
            flops=2 * tokens * depth * width,
            bytes_accessed=2 * (tokens * depth + width * (depth + tokens)),
            transcendentals=0,
        ),
        name="forward_sent",
    )(quarter, rows, weight)


def place_kernel(jx, ny, plan, mixed, has_extra, table, rows, weight, *rest):
    rest = list(rest)
    extra = rest.pop(0) if has_extra else None
    stage, sems = rest[-2:]
    outs = rest[-2 - sum(len(group[3]) for group in plan) : -2]
    step, steps = pl.program_id(0), pl.num_programs(0)
    tile = weight.shape[1]
    acc = jnp.dot(rows[...], weight[...], preferred_element_type=F32)
    if has_extra:
        acc = acc + extra[...].astype(F32)
    stage[step] = acc.astype(BF16)

    def copies(at, act):
        columns = pl.ds(pl.multiple_of(at * tile, 128), tile)
        for g, (first, stride, size, numbers) in enumerate(plan):
            for jy in range(ny):

                def copy(k1, k2, first=first + jy * stride, size=size, numbers=numbers, g=g, jy=jy):
                    act(
                        pltpu.make_async_copy(
                            stage.at[at, pl.ds(first, size), :],
                            outs[numbers[k1]].at[k2, :, columns],
                            sems.at[at, g * ny + jy],
                        )
                    )

                if not mixed or jx == jy:
                    copy(jx, jy)
                else:
                    pl.when(table[1] == 0)(functools.partial(copy, jx, jy))
                    pl.when(table[1] != 0)(functools.partial(copy, jy, jx))

    copies(step, lambda copy: copy.start())

    @pl.when(step == steps - 1)
    def _():
        for at in range(stage.shape[0]):
            copies(at, lambda copy: copy.wait())


def forward_placed(rows, weight, quarter, extra, jx, swapped, places, size, at, before):
    tokens, depth = rows.shape
    width = weight.shape[1] // at.owners
    tile = tile_of(width, 768)
    per = width // tile
    plan, shapes = [], []
    for first, stride in places:
        plan.append((first, stride, size, [len(shapes) + k for k in range(at.nx)]))
        shapes += [jax.ShapeDtypeStruct((at.ny, size, width), BF16)] * at.nx
    specs = [
        pl.BlockSpec((tokens, depth), lambda j, t: (0, 0)),
        pl.BlockSpec((depth, tile), lambda j, t: (0, t[0] * per + j)),
    ]
    operands = [rows, weight]
    if extra is not None:
        specs.append(pl.BlockSpec((tokens, tile), lambda j, t: (0, j)))
        operands.append(extra)
    aliases = {}
    if before is not None:
        aliases = {1 + len(operands) + i: i for i in range(len(shapes))}
        specs += [pl.BlockSpec(memory_space=pltpu.HBM)] * len(shapes)
        operands += list(before)
    return pl.pallas_call(
        functools.partial(place_kernel, jx, at.ny, plan, at.mixed, extra is not None),
        grid_spec=pltpu.PrefetchScalarGridSpec(
            num_scalar_prefetch=1,
            grid=(per,),
            in_specs=specs,
            out_specs=[pl.BlockSpec(memory_space=pltpu.HBM)] * len(shapes),
            scratch_shapes=[
                pltpu.VMEM((per, tokens, tile), BF16),
                pltpu.SemaphoreType.DMA((per, len(places) * at.ny)),
            ],
        ),
        out_shape=shapes,
        input_output_aliases=aliases,
        compiler_params=pltpu.CompilerParams(vmem_limit_bytes=VMEM),
        cost_estimate=pl.CostEstimate(
            flops=2 * tokens * depth * width,
            bytes_accessed=2 * (tokens * depth + width * (depth + 2 * tokens)),
            transcendentals=0,
        ),
        name="forward_placed",
    )(jnp.concatenate([quarter, swapped]), *operands)


def gather_kernel(plan, swapped, *rest):
    sources = max(item[0] for item in plan) + 1
    blocks, (out, stage, loads, stores) = rest[:sources], rest[-4:]
    copies, done = [], 0
    for i, (number, index, (j1, j2), first, stride, size) in enumerate(plan):
        jy = jnp.where(swapped[0] == 0, j1, j2)
        jx = jnp.where(swapped[0] == 0, j2, j1)
        place = stage.at[pl.ds(done, size)]
        done += size
        row = pl.multiple_of(first + jy * stride, 128)
        copies.append(
            (
                pltpu.make_async_copy(blocks[number].at[index], place, loads.at[i]),
                pltpu.make_async_copy(place, out.at[jx, pl.ds(row, size)], stores.at[i]),
            )
        )
    for load, _ in copies:
        load.start()
    for load, store in copies:
        load.wait()
        store.start()
    for _, store in copies:
        store.wait()


def put_together(plan, blocks, swapped, shape):
    operands = list(blocks)
    return pl.pallas_call(
        functools.partial(gather_kernel, plan),
        grid_spec=pltpu.PrefetchScalarGridSpec(
            num_scalar_prefetch=1,
            grid=(1,),
            in_specs=[pl.BlockSpec(memory_space=pl.ANY)] * len(operands),
            out_specs=pl.BlockSpec(memory_space=pltpu.HBM),
            scratch_shapes=[
                pltpu.VMEM((sum(item[5] for item in plan), shape[-1]), BF16),
                pltpu.SemaphoreType.DMA((len(plan),)),
                pltpu.SemaphoreType.DMA((len(plan),)),
            ],
        ),
        out_shape=jax.ShapeDtypeStruct(shape, BF16),
        compiler_params=pltpu.CompilerParams(vmem_limit_bytes=VMEM),
        cost_estimate=pl.CostEstimate(
            flops=0, bytes_accessed=4 * sum(b.size for b in blocks), transcendentals=0
        ),
        name="put_together",
    )(swapped, *operands)


def weight_kernel(sources, quarters, turned, *rest):
    total, first = None, 0
    for block in rest[:sources]:
        size = block.shape[1]
        part = jnp.dot(turned[:, first : first + size], block[0], preferred_element_type=F32)
        total = part if total is None else total + part
        first += size
    rest[-1][...] = total.astype(BF16)


def weight_gradient(turned, grads, jx, quarter, shape, before):
    depth, tokens = turned.shape
    width = grads[0].shape[2]
    tile = tile_of(width, 768)
    per = width // tile
    specs = [pl.BlockSpec((depth, tokens), lambda j, q: (0, 0))]
    for block in grads:
        specs.append(pl.BlockSpec((1, block.shape[1], tile), lambda j, q: (jx, 0, j)))
    operands = [turned] + list(grads)
    aliases = {}
    if before is not None:
        specs.append(pl.BlockSpec(memory_space=pltpu.HBM))
        aliases = {len(operands) + 1: 0}
        operands.append(before)
    return pl.pallas_call(
        functools.partial(weight_kernel, len(grads)),
        grid_spec=pltpu.PrefetchScalarGridSpec(
            num_scalar_prefetch=1,
            grid=(per,),
            in_specs=specs,
            out_specs=pl.BlockSpec((depth, tile), lambda j, q: (0, q[0] * per + j)),
        ),
        out_shape=jax.ShapeDtypeStruct(shape, BF16),
        input_output_aliases=aliases,
        compiler_params=pltpu.CompilerParams(vmem_limit_bytes=VMEM),
        cost_estimate=pl.CostEstimate(
            flops=2 * tokens * depth * width,
            bytes_accessed=2 * (tokens * depth + width * (depth + tokens)),
            transcendentals=0,
        ),
        name="weight_gradient",
    )(quarter, *operands)


def hidden_kernel(steps, each, last, table, gates, weight, *rest):
    out, total = rest[-2:]
    sources = steps // each
    step = pl.program_id(0)

    @pl.when(step == 0)
    def _():
        total[...] = jnp.zeros_like(total)

    for i, block in enumerate(rest[:sources]):

        @pl.when(step // each == i)
        def _(block=block):
            total[...] += lax.dot_general(
                block[0], weight[...], (((1,), (1,)), ((), ())), preferred_element_type=F32
            )

    @pl.when(step == steps - 1)
    def _():
        back = (total[...] * gates[...]).astype(BF16)
        if last:
            chosen, before = rest[sources : sources + 2]
            size = before.shape[0]
            picked = jnp.dot(chosen[:, :size], before[...], preferred_element_type=F32)
            picked += jnp.dot(chosen[:, size:], back, preferred_element_type=F32)
            out[...] = picked.astype(BF16)
        else:
            out[...] = back


def hidden_gradient(gates, grads, weight, quarters, chosen=None, before=None):
    count, tokens, width = grads[0].shape
    depth = weight.shape[0]
    tile = tile_of(width, 1536)
    per = width // tile
    each = per * count
    steps = each * len(grads)
    last = chosen is not None
    height = chosen.shape[0] if last else tokens
    specs = [
        pl.BlockSpec((tokens, 1), lambda s, t: (0, 0)),
        pl.BlockSpec((depth, tile), lambda s, t: (0, t[s // per] * per + s % per)),
    ]
    for i in range(len(grads)):

        def place(s, t, i=i):
            s = jnp.clip(s - i * each, 0, each - 1)
            return (s // per, 0, s % per)

        specs.append(pl.BlockSpec((1, tokens, tile), place))
    operands = [gates, weight] + list(grads)
    flops = 2 * tokens * depth * width * count * len(grads)
    if last:
        specs.append(pl.BlockSpec(chosen.shape, lambda s, t: (0, 0)))
        specs.append(pl.BlockSpec(before.shape, lambda s, t: (0, 0)))
        operands += [chosen, before]
        flops += 2 * chosen.shape[0] * chosen.shape[1] * depth
    return pl.pallas_call(
        functools.partial(hidden_kernel, steps, each, last),
        grid_spec=pltpu.PrefetchScalarGridSpec(
            num_scalar_prefetch=1,
            grid=(steps,),
            in_specs=specs,
            out_specs=pl.BlockSpec((height, depth), lambda s, t: (0, 0)),
            scratch_shapes=[pltpu.VMEM((tokens, depth), F32)],
        ),
        out_shape=jax.ShapeDtypeStruct((height, depth), BF16),
        compiler_params=pltpu.CompilerParams(vmem_limit_bytes=VMEM),
        cost_estimate=pl.CostEstimate(
            flops=flops,
            bytes_accessed=2 * len(grads) * count * width * (depth + tokens),
            transcendentals=0,
        ),
        name="hidden_gradient",
    )(quarters, *operands)


def tie(value, *others):
    return lax.optimization_barrier((value, others))[0]


def body(hidden, down_weight, grad_out, routing, gates):
    at = Layout()
    nx, ny, nz = at.nx, at.ny, at.nz
    rows, width = grad_out.shape
    top = routing.shape[1]
    slots = hidden.shape[1]
    capacity = slots // at.groups
    hidden_rows, weight = hidden[0], down_weight[0]

    turns = [list(range(nz // 2)), list(range(nz // 2, nz))]
    order = [(jz, jy) for turn in turns for jy in range(ny) for jz in turn]
    half = len(turns[0]) * ny * rows
    places = [
        (base + i * rows, len(turn) * rows)
        for base, turn in zip((0, half), turns)
        for i in range(len(turn))
    ]
    swapped = ((at.core == 1) if at.mixed else (at.core < 0)).astype(jnp.int32)[None]
    back_x = (at.x - jnp.arange(nx)) % nx * at.nc
    mine = (back_x + at.core).astype(jnp.int32)
    theirs = (back_x + (at.core + at.nc - 1) % at.nc).astype(jnp.int32)
    two = at.nc > 1
    quarters = jnp.concatenate([mine, theirs]) if two else mine

    def share(block, name):
        with jax.named_scope(name):
            return at.ring_c.shift(block) if two else block

    def gathered(ring, block, name):
        with jax.named_scope(name):
            return ring.gather(block)

    def shifted(k, block, name):
        with jax.named_scope(name):
            return at.far_z[k % nz].shift(block)

    packed = jnp.concatenate([routing.astype(F32).T, gates.T])
    packed = jnp.stack(gathered(at.ring_y, packed, "routes_y"))
    plane = [grad_out]
    first = [gathered(at.ring_1, grad_out, "own_first")]
    tables = [packed] + [shifted(jz, packed, "routes_z") for jz in range(1, nz)]
    plane.append(shifted(1, tie(grad_out, packed), "plane_1"))
    second = [gathered(at.ring_2, jnp.stack(first[0]), "own_second")]
    packed = jnp.stack([tables[jz][jy] for jz, jy in order])

    hits = packed[:, :top] == lax.axis_index("expert").astype(F32)
    hit = hits.astype(F32).sum(axis=1)
    gate = jnp.where(hits, packed[:, top:], 0.0).sum(axis=1)
    earlier = (jnp.arange(rows)[:, None] < jnp.arange(rows)[None, :]).astype(BF16)
    place = jnp.dot(hit.astype(BF16), earlier, preferred_element_type=F32).astype(jnp.int32)
    shards = jnp.stack([(at.z - jz) % nz * ny + (at.y - jy) % ny for jz, jy in order])
    slot_of = jnp.where(hit > 0, place + shards[:, None] * capacity, -1).reshape(-1)
    numbers = jnp.arange(slots, dtype=jnp.int32)
    chosen = (slot_of[:, None] == numbers[None, :]).astype(BF16)
    chosen_turned = (numbers[:, None] == slot_of[None, :]).astype(BF16)
    gate_column = gate.reshape(-1)[:, None]
    rows_in = jnp.dot(chosen, hidden_rows, preferred_element_type=F32)
    rows_in = (rows_in * gate_column).astype(BF16)

    plane.append(shifted(1, plane[1], "plane_2"))
    first.append(gathered(at.ring_1, plane[1], "plane_1_first"))
    ask = tie(theirs, plane[1], first[0])
    sent = []
    if two:
        sent = [forward_sent(rows_in, weight, ask[:1])]
    plane[2], first[1] = tie((plane[2], first[1]), sent)
    plane.append(shifted(1, plane[2], "plane_3"))
    first.append(gathered(at.ring_1, plane[2], "plane_2_first"))
    first[1] = jnp.stack(first[1])
    second.append(gathered(at.ring_2, first[1], "plane_1_second"))
    ask = tie(theirs, first[1], plane[2])
    if two:
        sent += [forward_sent(rows_in, weight, ask[jx : jx + 1]) for jx in range(1, nx)]
    extras = [share(block, "forward_core") for block in sent] if two else [None] * nx
    first[2] = jnp.stack(tie(first[2], sent[1:]))
    second.append(gathered(at.ring_2, first[2], "plane_2_second"))
    ask = tie(mine, first[2])
    placed = forward_placed(
        rows_in, weight, ask[:1], extras[0], 0, swapped, places, rows, at, None
    )
    plane[3], placed = tie((plane[3], placed), placed)
    first.append(gathered(at.ring_1, plane[3], "plane_3_first"))
    ask = tie(mine, plane[3])
    for jx in range(1, nx):
        placed = forward_placed(
            rows_in, weight, ask[jx : jx + 1], extras[jx], jx, swapped, places, rows, at, placed
        )
    first[3], second[0], second[1] = tie((first[3], second[0], second[1]), placed)
    first[3] = jnp.stack(first[3])
    second.append(gathered(at.ring_2, first[3], "plane_3_second"))

    def assembled(turn):
        plan, blocks = [], []
        for i, jz in enumerate(turn):
            for j2 in range(nx):
                for j1 in range(ny):
                    item = (len(blocks), j1, (j1, j2), i * rows, len(turn) * rows, rows)
                    plan.append(item)
                blocks.append(second[jz][j2])
        return put_together(plan, blocks, swapped, (nx, half, width))

    class Sum:
        def __init__(self, jz):
            self.name = "sum_%d" % jz
            self.terms = list(placed[jz * nx : (jz + 1) * nx])

        def start(self, ring, after=()):
            with jax.named_scope(self.name):
                self.terms = tie(self.terms, after)
                total = self.terms[1]
                for j in range(2, ring.size):
                    total = self.terms[j] + ring.shift(total)
                self.sent = total
                self.got = ring.shift(total)

        def finish(self, after):
            self.terms = self.terms[0] + tie(self.got, after)

        def second(self):
            self.terms = [self.terms[j] for j in range(ny)]
            self.start(at.ring_1)

    sums = [Sum(jz) for jz in range(nz)]
    sums[2].start(at.ring_2)
    grads_1 = assembled(turns[0])
    others_1 = [grads_1, share(grads_1, "gradients_core")] if two else [grads_1]
    sums[3].start(at.ring_2, grads_1)
    ask = tie(quarters, first[3], sums[3].sent)
    back = hidden_gradient(gate_column[:half], others_1, weight, ask)

    second[2], second[3] = tie((second[2], second[3]), back)
    grads_2 = assembled(turns[1])
    others_2 = [grads_2, share(grads_2, "gradients_core")] if two else [grads_2]
    sums[1].start(at.ring_2, grads_2)
    turned = rows_in.T
    ask = tie(mine, sums[1].sent)
    pair = [grads_1, grads_2]
    grad_weight = weight_gradient(turned, pair, 0, ask[:1], weight.shape, None)
    sums[2].finish(grad_weight)
    sums[2].second()
    ask = tie(quarters, sums[2].sent)
    grad_hidden = hidden_gradient(
        gate_column[half:], others_2, weight, ask, chosen_turned, back
    )

    received = {}
    sums[2].finish(grad_hidden)
    received[2] = shifted(nz - 2, sums[2].terms, "sum_2_z")
    sums[3].finish(grad_hidden)
    sums[3].second()
    sums[0].start(at.ring_2, grad_hidden)
    ask = tie(mine, sums[3].sent, sums[2].terms, sums[0].sent)
    for jx in range(1, nx):
        grad_weight = weight_gradient(
            turned, pair, jx, ask[jx : jx + 1], weight.shape, grad_weight
        )
    sums[3].finish(grad_weight)
    received[3] = shifted(nz - 3, sums[3].terms, "sum_3_z")
    sums[1].finish(grad_weight)
    sums[1].second()
    ask = tie(theirs, sums[3].terms, sums[1].sent)
    pair = [others_1[-1], others_2[-1]]
    for jx in range(nx if two else 0):
        grad_weight = weight_gradient(
            turned, pair, jx, ask[jx : jx + 1], weight.shape, grad_weight
        )
        if jx == 0:
            sums[1].finish(grad_weight)
            received[1] = shifted(nz - 1, sums[1].terms, "sum_1_z")
            sums[0].finish(grad_weight)
            sums[0].second()
            ask = tie(theirs, sums[1].terms, sums[0].sent)
    if not two:
        sums[1].finish(grad_weight)
        received[1] = shifted(nz - 1, sums[1].terms, "sum_1_z")
        sums[0].finish(grad_weight)
        sums[0].second()
    sums[0].finish(grad_weight)
    mixed_out = sums[0].terms.astype(F32)
    for jz in range(1, nz):
        mixed_out = mixed_out + tie(received[jz], grad_weight).astype(F32)
    return (mixed_out.astype(BF16), grad_hidden[None], grad_weight[None])


def solution(mesh):
    return jax.shard_map(
        body,
        mesh=mesh,
        in_specs=(
            P("expert", None, "dp"),
            P("expert", "dp", None),
            P("dp", "expert"),
            P("dp", None),
            P("dp", None),
        ),
        out_specs=(P("dp", "expert"), P("expert", None, "dp"), P("expert", "dp", None)),
        check_vma=False,
    )
```

```python
import functools
import jax
import jax.numpy as jnp
from jax import lax
from jax.experimental import pallas as pl
from jax.experimental.pallas import tpu as pltpu
from jax.sharding import PartitionSpec as P

BF16, F32 = jnp.bfloat16, jnp.float32
ALL = ("dp", "expert")
VMEM = 44 * 2**20


def cost(flops, moved):
    return pl.CostEstimate(flops=flops, bytes_accessed=moved, transcendentals=0)


class Ring:
    def __init__(self, size, perm):
        self.size, self.perm = size, perm

    def shift(self, block):
        return lax.ppermute(block, ALL, self.perm)

    def gather(self, block):
        blocks = [block]
        for _ in range(self.size - 1):
            blocks.append(self.shift(blocks[-1]))
        return blocks

    def scatter(self, blocks):
        if self.size == 1:
            return blocks[0]
        total = blocks[1]
        for j in list(range(2, self.size)) + [0]:
            total = blocks[j] + self.shift(total)
        return total


class Layout:
    def __init__(self):
        self.groups, self.owners = lax.axis_size("dp"), lax.axis_size("expert")
        self.nc = 2 if self.owners % 2 == 0 else 1
        self.nx = self.owners // self.nc
        self.ny = self.nx if self.groups % self.nx == 0 else 1
        self.nz = self.groups // self.ny
        dp, expert = lax.axis_index("dp"), lax.axis_index("expert")
        self.z, self.y = dp // self.ny, dp % self.ny
        self.x, self.core = expert // self.nc, expert % self.nc
        self.mixed = self.nx == self.ny and self.nc == 2
        step = {
            "x": lambda z, y, x, c: (z, y, (x + 1) % self.nx, c),
            "y": lambda z, y, x, c: (z, (y + 1) % self.ny, x, c),
            "c": lambda z, y, x, c: (z, y, x, (c + 1) % self.nc),
        }
        swapped = lambda c: self.mixed and c == 1
        self.far_z = [
            self.ring(self.nz, lambda z, y, x, c, k=k: ((z + k) % self.nz, y, x, c))
            for k in range(self.nz)
        ]
        self.ring_y = self.ring(self.ny, step["y"])
        self.ring_c = self.ring(self.nc, step["c"])
        self.ring_1 = self.ring(
            self.ny, lambda z, y, x, c: step["x" if swapped(c) else "y"](z, y, x, c)
        )
        self.ring_2 = self.ring(
            self.nx, lambda z, y, x, c: step["y" if swapped(c) else "x"](z, y, x, c)
        )

    def ring(self, size, onward):
        flat = lambda z, y, x, c: ((z * self.ny + y) * self.nx + x) * self.nc + c
        perm = []
        for z in range(self.nz):
            for y in range(self.ny):
                for x in range(self.nx):
                    for c in range(self.nc):
                        perm.append((flat(z, y, x, c), flat(*onward(z, y, x, c))))
        return Ring(size, perm)


def tile_of(width, most):
    tile = most
    while width % tile:
        tile -= 128
    return tile


def rows_kernel(size, shards, slots, gates, *rest):
    hidden, (out, turned) = rest[:-2], rest[-2:]
    count = shards.shape[0]
    capacity = hidden[0].shape[0] // count
    numbers = lax.broadcasted_iota(jnp.int32, (size, capacity), 1)
    for e, source in enumerate(hidden):
        slot_columns, gate_columns = slots[e].T, gates[e].T
        for i in range(count):
            block = source[pl.ds(pl.multiple_of(shards[i] * capacity, capacity), capacity), :]
            chosen = (slot_columns[:, i : i + 1] == numbers).astype(F32).astype(BF16)
            picked = jnp.dot(chosen, block, preferred_element_type=F32)
            picked = (picked * gate_columns[:, i : i + 1]).astype(BF16)
            out[e, pl.ds(i * size, size), :] = picked
            if e == 0:
                turned[:, pl.ds(i * size, size)] = picked.T


def token_rows(slot_of, gates, hidden, shards):
    experts, count, size = gates.shape
    tokens = count * size
    slots, depth = hidden[0].shape
    tile = tile_of(depth, 512)
    narrow = pl.BlockSpec((experts, count, size), lambda j, t: (0, 0, 0))
    return pl.pallas_call(
        functools.partial(rows_kernel, size),
        grid_spec=pltpu.PrefetchScalarGridSpec(
            num_scalar_prefetch=1,
            grid=(depth // tile,),
            in_specs=[narrow, narrow]
            + [pl.BlockSpec((slots, tile), lambda j, t: (0, j)) for _ in hidden],
            out_specs=[
                pl.BlockSpec((experts, tokens, tile), lambda j, t: (0, 0, j)),
                pl.BlockSpec((tile, tokens), lambda j, t: (j, 0)),
            ],
        ),
        out_shape=[
            jax.ShapeDtypeStruct((experts, tokens, depth), BF16),
            jax.ShapeDtypeStruct((depth, tokens), BF16),
        ],
        compiler_params=pltpu.CompilerParams(vmem_limit_bytes=VMEM),
        cost_estimate=cost(2 * tokens * slots * depth, 4 * experts * tokens * depth),
        name="token_rows",
    )(shards, slot_of, gates, *hidden)


def place_kernel(jx, first_tile, ny, plan, mixed, experts, table, rows, *rest):
    weights = rest[:experts]
    stage, sems = rest[-2:]
    outs = rest[-2 - sum(len(group[3]) for group in plan) : -2]
    step, steps = pl.program_id(0), pl.num_programs(0)
    tile = weights[0].shape[1]
    acc = jnp.dot(rows[0], weights[0][...], preferred_element_type=F32)
    for e in range(1, experts):
        acc = acc + jnp.dot(rows[e], weights[e][...], preferred_element_type=F32)
    stage[step] = acc.astype(BF16)

    def copies(at, act):
        columns = pl.ds(pl.multiple_of((first_tile + at) * tile, 128), tile)
        for g, (first, stride, size, numbers) in enumerate(plan):
            for jy in range(ny):

                def copy(k1, k2, first=first + jy * stride, size=size, numbers=numbers, g=g, jy=jy):
                    act(
                        pltpu.make_async_copy(
                            stage.at[at, pl.ds(first, size), :],
                            outs[numbers[k1]].at[k2, :, columns],
                            sems.at[at, g * ny + jy],
                        )
                    )

                if not mixed or jx == jy:
                    copy(jx, jy)
                else:
                    pl.when(table[1] == 0)(functools.partial(copy, jx, jy))
                    pl.when(table[1] != 0)(functools.partial(copy, jy, jx))

    copies(step, lambda copy: copy.start())

    @pl.when(step == steps - 1)
    def _():
        for at in range(stage.shape[0]):
            copies(at, lambda copy: copy.wait())


def forward_placed(rows, weights, table, jx, part, parts, places, size, at, before):
    experts, tokens, depth = rows.shape
    width = weights[0].shape[1] // at.owners
    tile = tile_of(width // parts, 384)
    per = width // parts // tile
    plan, shapes = [], []
    for first, stride in places:
        plan.append((first, stride, size, [len(shapes) + k for k in range(at.nx)]))
        shapes += [jax.ShapeDtypeStruct((at.ny, size, width), BF16)] * at.nx
    block = pl.BlockSpec((depth, tile), lambda j, t: (0, (t[0] * parts + part) * per + j))
    specs = [pl.BlockSpec((experts, tokens, depth), lambda j, t: (0, 0, 0))] + [block] * experts
    operands = [rows] + list(weights)
    aliases = {}
    if before is not None:
        aliases = {1 + len(operands) + i: i for i in range(len(shapes))}
        specs += [pl.BlockSpec(memory_space=pltpu.HBM)] * len(shapes)
        operands += list(before)
    return pl.pallas_call(
        functools.partial(place_kernel, jx, part * per, at.ny, plan, at.mixed, experts),
        grid_spec=pltpu.PrefetchScalarGridSpec(
            num_scalar_prefetch=1,
            grid=(per,),
            in_specs=specs,
            out_specs=[pl.BlockSpec(memory_space=pltpu.HBM)] * len(shapes),
            scratch_shapes=[
                pltpu.VMEM((per, tokens, tile), BF16),
                pltpu.SemaphoreType.DMA((per, len(places) * at.ny)),
            ],
        ),
        out_shape=shapes,
        input_output_aliases=aliases,
        compiler_params=pltpu.CompilerParams(vmem_limit_bytes=VMEM),
        cost_estimate=cost(
            2 * experts * tokens * depth * tile * per, 2 * tile * per * (2 * depth + 2 * tokens)
        ),
        name="forward_placed",
    )(table, *operands)


def gather_kernel(plan, outputs, swapped, *rest):
    sources = max(item[0] for item in plan) + 1
    blocks, outs, (stage, loads, stores) = rest[:sources], rest[-3 - outputs : -3], rest[-3:]
    places, done = [], 0
    for i, (number, index, _, _, _, size) in enumerate(plan):
        places.append(stage.at[pl.ds(done, size)])
        done += size
        pltpu.make_async_copy(blocks[number].at[index], places[i], loads.at[i]).start()

    def store(i, act):
        _, _, (j1, j2), first, stride, size = plan[i]

        def copy(jy, jx):
            target = outs[jx].at[pl.ds(first + jy * stride, size)]
            act(pltpu.make_async_copy(places[i], target, stores.at[i]))

        if j1 == j2:
            copy(j1, j2)
        else:
            pl.when(swapped[0] == 0)(functools.partial(copy, j1, j2))
            if max(j1, j2) < outputs:
                pl.when(swapped[0] != 0)(functools.partial(copy, j2, j1))

    for i, (number, index, _, _, _, size) in enumerate(plan):
        pltpu.make_async_copy(blocks[number].at[index], places[i], loads.at[i]).wait()
        store(i, lambda copy: copy.start())
    for i in range(len(plan)):
        store(i, lambda copy: copy.wait())


def put_together(plan, blocks, swapped, count, shape):
    return pl.pallas_call(
        functools.partial(gather_kernel, plan, count),
        grid_spec=pltpu.PrefetchScalarGridSpec(
            num_scalar_prefetch=1,
            grid=(1,),
            in_specs=[pl.BlockSpec(memory_space=pl.ANY)] * len(blocks),
            out_specs=[pl.BlockSpec(memory_space=pltpu.HBM)] * count,
            scratch_shapes=[
                pltpu.VMEM((sum(item[5] for item in plan), shape[-1]), BF16),
                pltpu.SemaphoreType.DMA((len(plan),)),
                pltpu.SemaphoreType.DMA((len(plan),)),
            ],
        ),
        out_shape=[jax.ShapeDtypeStruct(shape, BF16)] * count,
        compiler_params=pltpu.CompilerParams(vmem_limit_bytes=VMEM),
        cost_estimate=cost(0, 4 * sum(b.size for b in blocks)),
        name="put_together",
    )(swapped, *blocks)


def weight_kernel(count, per, quarters, turned, *rest):
    sources = (len(rest) - 1) // count
    step = pl.program_id(0)
    for i in range(count):

        @pl.when(step // per == i)
        def _(i=i):
            total, first = None, 0
            for block in rest[i * sources : (i + 1) * sources]:
                size = block.shape[0]
                part = jnp.dot(
                    turned[:, first : first + size], block[...], preferred_element_type=F32
                )
                total = part if total is None else total + part
                first += size
            rest[-1][...] = total.astype(BF16)


def weight_gradient(turned, grads, quarters, shape, before):
    depth, tokens = turned.shape
    count = len(grads)
    width = grads[0][0].shape[1]
    tile = tile_of(width, 768)
    per = width // tile
    specs = [pl.BlockSpec((depth, tokens), lambda j, q: (0, 0))]
    operands = [turned]
    for i in range(count):
        for block in grads[i]:
            specs.append(
                pl.BlockSpec(
                    (block.shape[0], tile), lambda j, q, i=i: (0, jnp.clip(j - i * per, 0, per - 1))
                )
            )
            operands.append(block)
    aliases, extra = {}, []
    kernel = functools.partial(weight_kernel, count, per)
    if before is not None:
        specs.append(pl.BlockSpec(memory_space=pltpu.HBM))
        aliases = {len(operands) + 1: 0}
        operands.append(before)
        inner = kernel
        kernel = lambda quarters, turned, *rest: inner(quarters, turned, *rest[:-2], rest[-1])
    return pl.pallas_call(
        kernel,
        grid_spec=pltpu.PrefetchScalarGridSpec(
            num_scalar_prefetch=1,
            grid=(count * per,),
            in_specs=specs,
            out_specs=pl.BlockSpec((depth, tile), lambda j, q: (0, q[j // per] * per + j % per)),
        ),
        out_shape=jax.ShapeDtypeStruct(shape, BF16),
        input_output_aliases=aliases,
        compiler_params=pltpu.CompilerParams(vmem_limit_bytes=VMEM),
        cost_estimate=cost(
            2 * tokens * depth * width * count, 2 * count * width * (depth + tokens)
        ),
        name="weight_gradient",
    )(quarters, *operands)


def hidden_kernel(steps, each, count, last, table, gates, slots, weight, *rest):
    out, total = rest[-2:]
    sources = steps // each
    step = pl.program_id(0)
    size = total.shape[0] // count

    @pl.when(step == 0)
    def _():
        total[...] = jnp.zeros_like(total)

    for i, block in enumerate(rest[:sources]):

        @pl.when(step // each == i)
        def _(block=block):
            total[...] += lax.dot_general(
                block[...], weight[...], (((1,), (1,)), ((), ())), preferred_element_type=F32
            )

    @pl.when(step == steps - 1)
    def _():
        capacity = out.shape[0] // (2 * count if last else count)
        numbers = lax.broadcasted_iota(jnp.int32, (capacity, size), 0)
        gate_columns = gates[...].T
        for i in range(count):
            span = pl.ds(i * size, size)
            back = (total[span, :] * gate_columns[:, i : i + 1]).astype(BF16)
            chosen = (slots[pl.ds(i, 1), :] == numbers).astype(F32).astype(BF16)
            picked = jnp.dot(chosen, back, preferred_element_type=F32).astype(BF16)
            if last:
                before = rest[sources]
                place = table[steps + count + i] * capacity
                out[pl.ds(pl.multiple_of(place, capacity), capacity), :] = picked
                place = table[steps + i] * capacity
                old = before[pl.ds(i * capacity, capacity), :]
                out[pl.ds(pl.multiple_of(place, capacity), capacity), :] = old
            else:
                out[pl.ds(i * capacity, capacity), :] = picked


def hidden_gradient(gates, slots, grads, weight, quarters, capacity, shards=None, before=None):
    tokens, width = grads[0].shape
    depth = weight.shape[0]
    tile = tile_of(width, 1536)
    per = width // tile
    steps = per * len(grads)
    last = before is not None
    number = slots.shape[0]
    height = capacity * number * (2 if last else 1)
    table = jnp.repeat(quarters, per) if per > 1 else quarters
    if last:
        table = jnp.concatenate([table, shards])
    specs = [
        pl.BlockSpec(gates.shape, lambda s, t: (0, 0)),
        pl.BlockSpec(slots.shape, lambda s, t: (0, 0)),
        pl.BlockSpec((depth, tile), lambda s, t: (0, t[s] * per + s % per)),
    ]
    for i in range(len(grads)):

        def place(s, t, i=i):
            return (0, jnp.clip(s - i * per, 0, per - 1))

        specs.append(pl.BlockSpec((tokens, tile), place))
    operands = [gates, slots, weight] + list(grads)
    if last:
        specs.append(pl.BlockSpec(before.shape, lambda s, t: (0, 0)))
        operands.append(before)
    return pl.pallas_call(
        functools.partial(hidden_kernel, steps, per, number, last),
        grid_spec=pltpu.PrefetchScalarGridSpec(
            num_scalar_prefetch=1,
            grid=(steps,),
            in_specs=specs,
            out_specs=pl.BlockSpec((height, depth), lambda s, t: (0, 0)),
            scratch_shapes=[pltpu.VMEM((tokens, depth), F32)],
        ),
        out_shape=jax.ShapeDtypeStruct((height, depth), BF16),
        compiler_params=pltpu.CompilerParams(vmem_limit_bytes=VMEM),
        cost_estimate=cost(2 * steps * tile * tokens * depth, 2 * steps * tile * (depth + tokens)),
        name="hidden_gradient",
    )(table, *operands)


def tie(value, *others):
    return lax.optimization_barrier((value, others))[0]


def body(hidden, down_weight, grad_out, routing, gates):
    at = Layout()
    nx, ny, nz = at.nx, at.ny, at.nz
    rows, width = grad_out.shape
    top = routing.shape[1]
    slots = hidden.shape[1]
    capacity = slots // at.groups
    hidden_rows, weight = hidden[0], down_weight[0]

    turns = [list(range(nz // 2)), list(range(nz // 2, nz))]
    order = [(jz, jy) for turn in turns for jy in range(ny) for jz in turn]
    size = len(turns[0]) * rows
    half = ny * size
    places = [(0, size), (half, size)]
    swapped = ((at.core == 1) if at.mixed else (at.core < 0)).astype(jnp.int32)[None]
    back_x = (at.x - jnp.arange(nx)) % nx * at.nc
    mine = (back_x + at.core).astype(jnp.int32)
    theirs = (back_x + (at.core + at.nc - 1) % at.nc).astype(jnp.int32)
    two = at.nc > 1
    quarters = jnp.concatenate([mine, theirs]) if two else mine

    def both(block, name):
        with jax.named_scope(name):
            return [block, at.ring_c.shift(block)] if two else [block]

    def gathered(ring, block, name):
        with jax.named_scope(name):
            return ring.gather(block)

    def shifted(k, block, name):
        with jax.named_scope(name):
            return at.far_z[k % nz].shift(block)

    packed = jnp.concatenate([routing.astype(F32).T, gates.T])
    packed = jnp.stack(gathered(at.ring_y, packed, "routes_y"))
    hiddens = both(hidden_rows, "hidden_core")
    plane = [grad_out]
    first = [gathered(at.ring_1, grad_out, "own_first")]
    tables = [packed] + [shifted(jz, packed, "routes_z") for jz in range(1, nz)]
    plane.append(shifted(1, tie(grad_out, packed), "plane_1"))
    first[0] = jnp.stack(first[0])
    weights = both(tie(weight, packed, hiddens), "weight_core")
    second = [gathered(at.ring_2, first[0], "own_second")]
    packed = jnp.stack([tables[jz][jy] for jz, jy in order])

    expert = lax.axis_index("expert")
    ours = [expert, expert - at.core + 1 - at.core] if two else [expert]
    ours = jnp.stack(ours).astype(F32)[:, None, None, None]
    hits = packed[None, :, :top] == ours
    hit = hits.astype(F32).sum(axis=2)
    gate = jnp.where(hits, packed[None, :, top:], 0.0).sum(axis=2)
    earlier = (jnp.arange(rows)[:, None] < jnp.arange(rows)[None, :]).astype(BF16)
    place = jnp.dot(hit.astype(BF16), earlier, preferred_element_type=F32).astype(jnp.int32)
    shards = jnp.stack([(at.z - jz) % nz * ny + (at.y - jy) % ny for jz, jy in order])
    shards = shards.astype(jnp.int32)
    slot_of = jnp.where(hit > 0, place, -1)
    rows_in, turned = token_rows(slot_of, gate, hiddens, shards)
    slot_of, gate = slot_of[0], gate[0]
    plane[1], first[0] = tie((plane[1], first[0]), rows_in)
    plane.append(shifted(1, plane[1], "plane_2"))
    plane.append(shifted(nz - 1, tie(grad_out, plane[1]), "plane_3"))
    first.append(gathered(at.ring_1, plane[1], "plane_1_first"))

    calls = [(jx, 0, 1) for jx in range(nx - 1)] + [(nx - 1, 0, 2), (nx - 1, 1, 2)]
    forward_tables = [jnp.concatenate([mine[jx : jx + 1], swapped]) for jx in range(nx)]

    def forward(call, placed, *after):
        jx, part, parts = call
        table = tie(forward_tables[jx], *after)
        return forward_placed(rows_in, weights, table, jx, part, parts, places, size, at, placed)

    first[1] = jnp.stack(first[1])
    second.append(gathered(at.ring_2, first[1], "plane_1_second"))
    done = None
    for call in calls[:-2]:
        done = forward(call, done, plane[1], first[1])
    pair = jnp.stack(tie(plane[2:], done))
    first.append(gathered(at.ring_1, pair, "pair_first"))

    def assembled(blocks, turn):
        plan = []
        for i in range(len(blocks) // nx):
            for j2 in range(nx):
                for j1 in range(ny):
                    number = i * nx + j2
                    plan.append((number, j1, (j1, j2), i * rows, size, blocks[number].shape[1]))
        return list(put_together(plan, blocks, swapped, nx, (half, width)))

    done = forward(calls[-2], done, pair, first[1])
    first[2] = jnp.stack(tie(first[2], done)).reshape(ny, size, width)
    second.append(gathered(at.ring_2, first[2], "pair_second"))
    grads_1 = assembled(tie(second[0] + second[1], done), turns[0])
    others_1 = [both(block, "gradients_core")[-1] for block in grads_1] if two else []
    placed = forward(calls[-1], done, first[2], grads_1)

    class Sum:
        def __init__(self, turn):
            self.name = "sum_%d" % turn
            self.terms = list(placed[turn * nx : (turn + 1) * nx])

        def start(self, ring, after=()):
            with jax.named_scope(self.name):
                self.terms = tie(self.terms, after)
                total = self.terms[1]
                for j in range(2, ring.size):
                    total = self.terms[j] + ring.shift(total)
                self.sent = total
                self.got = ring.shift(total)

        def finish(self, after):
            self.terms = self.terms[0] + tie(self.got, after)

        def second(self):
            self.terms = [self.terms[j] for j in range(ny)]
            self.start(at.ring_1)

    near, far = Sum(0), Sum(1)
    far.start(at.ring_2)
    ask = tie(quarters, far.sent)
    count = len(order) // 2
    back = hidden_gradient(gate[:count], slot_of[:count], grads_1 + others_1, weight, ask, capacity)

    grads_2 = assembled(tie(second[2], back), turns[1])
    others_2 = [both(block, "gradients_core")[-1] for block in grads_2] if two else []
    ask = tie(mine, grads_2)
    grad_weight = weight_gradient(turned, list(zip(grads_1, grads_2)), ask, weight.shape, None)
    far.finish(grad_weight)
    far.second()
    near.start(at.ring_2)
    ask = tie(quarters, far.sent, near.sent)
    grad_hidden = hidden_gradient(
        gate[count:],
        slot_of[count:],
        grads_2 + others_2,
        weight,
        ask,
        capacity,
        shards,
        back,
    )
    far.finish(grad_hidden)
    near.finish(grad_hidden)
    near.second()
    last = shifted(nz - 3, far.terms[rows:], "sum_3_z")
    onward = shifted(nz - 1, far.terms[:rows], "sum_2_z")
    ask = tie(theirs, far.terms, near.sent)
    if two:
        grad_weight = weight_gradient(
            turned, list(zip(others_1, others_2)), ask, weight.shape, grad_weight
        )
    near.finish(grad_weight)
    onward = tie(onward, grad_weight) + near.terms[rows:]
    onward = shifted(nz - 1, onward, "sum_1_z")
    mixed_out = near.terms[:rows].astype(F32) + last.astype(F32) + onward.astype(F32)
    return (mixed_out.astype(BF16), grad_hidden[None], grad_weight[None])


def solution(mesh):
    return jax.shard_map(
        body,
        mesh=mesh,
        in_specs=(
            P("expert", None, "dp"),
            P("expert", "dp", None),
            P("dp", "expert"),
            P("dp", None),
            P("dp", None),
        ),
        out_specs=(P("dp", "expert"), P("expert", None, "dp"), P("expert", "dp", None)),
        check_vma=False,
    )
```

```python
import functools
import jax
import jax.numpy as jnp
from jax import lax
from jax.experimental import pallas as pl
from jax.experimental.pallas import tpu as pltpu
from jax.sharding import PartitionSpec as P

BF16, F32 = jnp.bfloat16, jnp.float32
ALL = ("dp", "expert")
VMEM = 44 * 2**20


def cost(flops, moved):
    return pl.CostEstimate(flops=flops, bytes_accessed=moved, transcendentals=0)


class Ring:
    def __init__(self, size, perm):
        self.size, self.perm = size, perm

    def shift(self, block):
        return lax.ppermute(block, ALL, self.perm)

    def gather(self, block):
        blocks = [block]
        for _ in range(self.size - 1):
            blocks.append(self.shift(blocks[-1]))
        return blocks

    def scatter(self, blocks):
        if self.size == 1:
            return blocks[0]
        total = blocks[1]
        for j in list(range(2, self.size)) + [0]:
            total = blocks[j] + self.shift(total)
        return total


class Layout:
    def __init__(self):
        self.groups, self.owners = lax.axis_size("dp"), lax.axis_size("expert")
        self.nc = 2 if self.owners % 2 == 0 else 1
        self.nx = self.owners // self.nc
        self.ny = self.nx if self.groups % self.nx == 0 else 1
        self.nz = self.groups // self.ny
        dp, expert = lax.axis_index("dp"), lax.axis_index("expert")
        self.z, self.y = dp // self.ny, dp % self.ny
        self.x, self.core = expert // self.nc, expert % self.nc
        self.mixed = self.nx == self.ny and self.nc == 2
        step = {
            "x": lambda z, y, x, c: (z, y, (x + 1) % self.nx, c),
            "y": lambda z, y, x, c: (z, (y + 1) % self.ny, x, c),
            "c": lambda z, y, x, c: (z, y, x, (c + 1) % self.nc),
        }
        swapped = lambda c: self.mixed and c == 1
        self.far_z = [
            self.ring(self.nz, lambda z, y, x, c, k=k: ((z + k) % self.nz, y, x, c))
            for k in range(self.nz)
        ]
        self.ring_y = self.ring(self.ny, step["y"])
        self.ring_c = self.ring(self.nc, step["c"])
        self.ring_1 = self.ring(
            self.ny, lambda z, y, x, c: step["x" if swapped(c) else "y"](z, y, x, c)
        )
        self.ring_2 = self.ring(
            self.nx, lambda z, y, x, c: step["y" if swapped(c) else "x"](z, y, x, c)
        )

    def ring(self, size, onward):
        flat = lambda z, y, x, c: ((z * self.ny + y) * self.nx + x) * self.nc + c
        perm = []
        for z in range(self.nz):
            for y in range(self.ny):
                for x in range(self.nx):
                    for c in range(self.nc):
                        perm.append((flat(z, y, x, c), flat(*onward(z, y, x, c))))
        return Ring(size, perm)


def tile_of(width, most):
    tile = most
    while width % tile:
        tile -= 128
    return tile


def rows_kernel(size, shards, slots, gates, *rest):
    hidden, (out, turned) = rest[:-2], rest[-2:]
    count = shards.shape[0]
    capacity = hidden[0].shape[0] // count
    numbers = lax.broadcasted_iota(jnp.int32, (size, capacity), 1)
    for e, source in enumerate(hidden):
        slot_columns, gate_columns = slots[e].T, gates[e].T
        for i in range(count):
            block = source[pl.ds(pl.multiple_of(shards[i] * capacity, capacity), capacity), :]
            chosen = (slot_columns[:, i : i + 1] == numbers).astype(F32).astype(BF16)
            picked = jnp.dot(chosen, block, preferred_element_type=F32)
            picked = (picked * gate_columns[:, i : i + 1]).astype(BF16)
            out[e, pl.ds(i * size, size), :] = picked
            if e == 0:
                turned[:, pl.ds(i * size, size)] = picked.T


def token_rows(slot_of, gates, hidden, shards):
    experts, count, size = gates.shape
    tokens = count * size
    slots, depth = hidden[0].shape
    tile = tile_of(depth, 512)
    narrow = pl.BlockSpec((experts, count, size), lambda j, t: (0, 0, 0))
    return pl.pallas_call(
        functools.partial(rows_kernel, size),
        grid_spec=pltpu.PrefetchScalarGridSpec(
            num_scalar_prefetch=1,
            grid=(depth // tile,),
            in_specs=[narrow, narrow]
            + [pl.BlockSpec((slots, tile), lambda j, t: (0, j)) for _ in hidden],
            out_specs=[
                pl.BlockSpec((experts, tokens, tile), lambda j, t: (0, 0, j)),
                pl.BlockSpec((tile, tokens), lambda j, t: (j, 0)),
            ],
        ),
        out_shape=[
            jax.ShapeDtypeStruct((experts, tokens, depth), BF16),
            jax.ShapeDtypeStruct((depth, tokens), BF16),
        ],
        compiler_params=pltpu.CompilerParams(vmem_limit_bytes=VMEM),
        cost_estimate=cost(2 * tokens * slots * depth, 4 * experts * tokens * depth),
        name="token_rows",
    )(shards, slot_of, gates, *hidden)


def place_kernel(jx, first_tile, ny, plan, mixed, experts, table, rows, *rest):
    weights = rest[:experts]
    stage, sems = rest[-2:]
    outs = rest[-2 - sum(len(group[3]) for group in plan) : -2]
    step, steps = pl.program_id(0), pl.num_programs(0)
    tile = weights[0].shape[1]
    acc = jnp.dot(rows[0], weights[0][...], preferred_element_type=F32)
    for e in range(1, experts):
        acc = acc + jnp.dot(rows[e], weights[e][...], preferred_element_type=F32)
    stage[step] = acc.astype(BF16)

    def copies(at, act):
        columns = pl.ds(pl.multiple_of((first_tile + at) * tile, 128), tile)
        for g, (first, stride, size, numbers) in enumerate(plan):
            for jy in range(ny):

                def copy(k1, k2, first=first + jy * stride, size=size, numbers=numbers, g=g, jy=jy):
                    act(
                        pltpu.make_async_copy(
                            stage.at[at, pl.ds(first, size), :],
                            outs[numbers[k1]].at[k2, :, columns],
                            sems.at[at, g * ny + jy],
                        )
                    )

                if not mixed or jx == jy:
                    copy(jx, jy)
                else:
                    pl.when(table[1] == 0)(functools.partial(copy, jx, jy))
                    pl.when(table[1] != 0)(functools.partial(copy, jy, jx))

    copies(step, lambda copy: copy.start())

    @pl.when(step == steps - 1)
    def _():
        for at in range(stage.shape[0]):
            copies(at, lambda copy: copy.wait())


def forward_placed(rows, weights, table, jx, part, parts, places, size, at, before):
    experts, tokens, depth = rows.shape
    width = weights[0].shape[1] // at.owners
    tile = tile_of(width // parts, 384)
    per = width // parts // tile
    plan, shapes = [], []
    for first, stride in places:
        plan.append((first, stride, size, [len(shapes) + k for k in range(at.nx)]))
        shapes += [jax.ShapeDtypeStruct((at.ny, size, width), BF16)] * at.nx
    block = pl.BlockSpec((depth, tile), lambda j, t: (0, (t[0] * parts + part) * per + j))
    specs = [pl.BlockSpec((experts, tokens, depth), lambda j, t: (0, 0, 0))] + [block] * experts
    operands = [rows] + list(weights)
    aliases = {}
    if before is not None:
        aliases = {1 + len(operands) + i: i for i in range(len(shapes))}
        specs += [pl.BlockSpec(memory_space=pltpu.HBM)] * len(shapes)
        operands += list(before)
    return pl.pallas_call(
        functools.partial(place_kernel, jx, part * per, at.ny, plan, at.mixed, experts),
        grid_spec=pltpu.PrefetchScalarGridSpec(
            num_scalar_prefetch=1,
            grid=(per,),
            in_specs=specs,
            out_specs=[pl.BlockSpec(memory_space=pltpu.HBM)] * len(shapes),
            scratch_shapes=[
                pltpu.VMEM((per, tokens, tile), BF16),
                pltpu.SemaphoreType.DMA((per, len(places) * at.ny)),
            ],
        ),
        out_shape=shapes,
        input_output_aliases=aliases,
        compiler_params=pltpu.CompilerParams(vmem_limit_bytes=VMEM),
        cost_estimate=cost(
            2 * experts * tokens * depth * tile * per, 2 * tile * per * (2 * depth + 2 * tokens)
        ),
        name="forward_placed",
    )(table, *operands)


def gather_kernel(plan, outputs, swapped, *rest):
    sources = max(item[0] for item in plan) + 1
    blocks, outs, (stage, loads, stores) = rest[:sources], rest[-3 - outputs : -3], rest[-3:]
    places, done = [], 0
    for i, (number, index, _, _, _, size) in enumerate(plan):
        places.append(stage.at[pl.ds(done, size)])
        done += size
        pltpu.make_async_copy(blocks[number].at[index], places[i], loads.at[i]).start()

    def store(i, act):
        _, _, (j1, j2), first, stride, size = plan[i]

        def copy(jy, jx):
            target = outs[jx].at[pl.ds(first + jy * stride, size)]
            act(pltpu.make_async_copy(places[i], target, stores.at[i]))

        if j1 == j2:
            copy(j1, j2)
        else:
            pl.when(swapped[0] == 0)(functools.partial(copy, j1, j2))
            if max(j1, j2) < outputs:
                pl.when(swapped[0] != 0)(functools.partial(copy, j2, j1))

    for i, (number, index, _, _, _, size) in enumerate(plan):
        pltpu.make_async_copy(blocks[number].at[index], places[i], loads.at[i]).wait()
        store(i, lambda copy: copy.start())
    for i in range(len(plan)):
        store(i, lambda copy: copy.wait())


def put_together(plan, blocks, swapped, count, shape):
    return pl.pallas_call(
        functools.partial(gather_kernel, plan, count),
        grid_spec=pltpu.PrefetchScalarGridSpec(
            num_scalar_prefetch=1,
            grid=(1,),
            in_specs=[pl.BlockSpec(memory_space=pl.ANY)] * len(blocks),
            out_specs=[pl.BlockSpec(memory_space=pltpu.HBM)] * count,
            scratch_shapes=[
                pltpu.VMEM((sum(item[5] for item in plan), shape[-1]), BF16),
                pltpu.SemaphoreType.DMA((len(plan),)),
                pltpu.SemaphoreType.DMA((len(plan),)),
            ],
        ),
        out_shape=[jax.ShapeDtypeStruct(shape, BF16)] * count,
        compiler_params=pltpu.CompilerParams(vmem_limit_bytes=VMEM),
        cost_estimate=cost(0, 4 * sum(b.size for b in blocks)),
        name="put_together",
    )(swapped, *blocks)


def weight_kernel(count, per, quarters, turned, *rest):
    sources = (len(rest) - 1) // count
    step = pl.program_id(0)
    for i in range(count):

        @pl.when(step // per == i)
        def _(i=i):
            total, first = None, 0
            for block in rest[i * sources : (i + 1) * sources]:
                size = block.shape[0]
                part = jnp.dot(
                    turned[:, first : first + size], block[...], preferred_element_type=F32
                )
                total = part if total is None else total + part
                first += size
            rest[-1][...] = total.astype(BF16)


def weight_gradient(turned, grads, quarters, shape, before):
    depth, tokens = turned.shape
    count = len(grads)
    width = grads[0][0].shape[1]
    tile = tile_of(width, 768)
    per = width // tile
    specs = [pl.BlockSpec((depth, tokens), lambda j, q: (0, 0))]
    operands = [turned]
    for i in range(count):
        for block in grads[i]:
            specs.append(
                pl.BlockSpec(
                    (block.shape[0], tile), lambda j, q, i=i: (0, jnp.clip(j - i * per, 0, per - 1))
                )
            )
            operands.append(block)
    aliases, extra = {}, []
    kernel = functools.partial(weight_kernel, count, per)
    if before is not None:
        specs.append(pl.BlockSpec(memory_space=pltpu.HBM))
        aliases = {len(operands) + 1: 0}
        operands.append(before)
        inner = kernel
        kernel = lambda quarters, turned, *rest: inner(quarters, turned, *rest[:-2], rest[-1])
    return pl.pallas_call(
        kernel,
        grid_spec=pltpu.PrefetchScalarGridSpec(
            num_scalar_prefetch=1,
            grid=(count * per,),
            in_specs=specs,
            out_specs=pl.BlockSpec((depth, tile), lambda j, q: (0, q[j // per] * per + j % per)),
        ),
        out_shape=jax.ShapeDtypeStruct(shape, BF16),
        input_output_aliases=aliases,
        compiler_params=pltpu.CompilerParams(vmem_limit_bytes=VMEM),
        cost_estimate=cost(
            2 * tokens * depth * width * count, 2 * count * width * (depth + tokens)
        ),
        name="weight_gradient",
    )(quarters, *operands)


def hidden_kernel(steps, each, count, last, table, gates, slots, weight, *rest):
    out, total = rest[-2:]
    sources = steps // each
    step = pl.program_id(0)
    size = total.shape[0] // count

    @pl.when(step == 0)
    def _():
        total[...] = jnp.zeros_like(total)

    for i, block in enumerate(rest[:sources]):

        @pl.when(step // each == i)
        def _(block=block):
            total[...] += lax.dot_general(
                block[...], weight[...], (((1,), (1,)), ((), ())), preferred_element_type=F32
            )

    @pl.when(step == steps - 1)
    def _():
        capacity = out.shape[0] // (2 * count if last else count)
        numbers = lax.broadcasted_iota(jnp.int32, (capacity, size), 0)
        gate_columns = gates[...].T
        for i in range(count):
            span = pl.ds(i * size, size)
            back = (total[span, :] * gate_columns[:, i : i + 1]).astype(BF16)
            chosen = (slots[pl.ds(i, 1), :] == numbers).astype(F32).astype(BF16)
            picked = jnp.dot(chosen, back, preferred_element_type=F32).astype(BF16)
            if last:
                before = rest[sources]
                place = table[steps // each + count + i] * capacity
                out[pl.ds(pl.multiple_of(place, capacity), capacity), :] = picked
                place = table[steps // each + i] * capacity
                old = before[pl.ds(i * capacity, capacity), :]
                out[pl.ds(pl.multiple_of(place, capacity), capacity), :] = old
            else:
                out[pl.ds(i * capacity, capacity), :] = picked


def hidden_gradient(gates, slots, grads, weight, table, capacity, before=None):
    tokens, width = grads[0].shape
    depth = weight.shape[0]
    tile = tile_of(width, 1536)
    per = width // tile
    steps = per * len(grads)
    last = before is not None
    number = slots.shape[0]
    height = capacity * number * (2 if last else 1)
    specs = [
        pl.BlockSpec(gates.shape, lambda s, t: (0, 0)),
        pl.BlockSpec(slots.shape, lambda s, t: (0, 0)),
        pl.BlockSpec((depth, tile), lambda s, t: (0, t[s // per] * per + s % per)),
    ]
    for i in range(len(grads)):

        def place(s, t, i=i):
            return (0, jnp.clip(s - i * per, 0, per - 1))

        specs.append(pl.BlockSpec((tokens, tile), place))
    operands = [gates, slots, weight] + list(grads)
    if last:
        specs.append(pl.BlockSpec(before.shape, lambda s, t: (0, 0)))
        operands.append(before)
    return pl.pallas_call(
        functools.partial(hidden_kernel, steps, per, number, last),
        grid_spec=pltpu.PrefetchScalarGridSpec(
            num_scalar_prefetch=1,
            grid=(steps,),
            in_specs=specs,
            out_specs=pl.BlockSpec((height, depth), lambda s, t: (0, 0)),
            scratch_shapes=[pltpu.VMEM((tokens, depth), F32)],
        ),
        out_shape=jax.ShapeDtypeStruct((height, depth), BF16),
        compiler_params=pltpu.CompilerParams(vmem_limit_bytes=VMEM),
        cost_estimate=cost(2 * steps * tile * tokens * depth, 2 * steps * tile * (depth + tokens)),
        name="hidden_gradient",
    )(table, *operands)


def tie(value, *others):
    return lax.optimization_barrier((value, others))[0]


def body(hidden, down_weight, grad_out, routing, gates):
    at = Layout()
    nx, ny, nz = at.nx, at.ny, at.nz
    rows, width = grad_out.shape
    top = routing.shape[1]
    slots = hidden.shape[1]
    capacity = slots // at.groups
    hidden_rows, weight = hidden[0], down_weight[0]

    turns = [list(range(nz // 2)), list(range(nz // 2, nz))]
    order = [(jz, jy) for turn in turns for jy in range(ny) for jz in turn]
    size = len(turns[0]) * rows
    half = ny * size
    places = [(0, size), (half, size)]
    swapped = ((at.core == 1) if at.mixed else (at.core < 0)).astype(jnp.int32)[None]
    back_x = (at.x - jnp.arange(nx)) % nx * at.nc
    mine = (back_x + at.core).astype(jnp.int32)
    theirs = (back_x + (at.core + at.nc - 1) % at.nc).astype(jnp.int32)
    two = at.nc > 1
    quarters = jnp.concatenate([mine, theirs]) if two else mine

    def both(block, name):
        with jax.named_scope(name):
            return [block, at.ring_c.shift(block)] if two else [block]

    def gathered(ring, block, name):
        with jax.named_scope(name):
            return ring.gather(block)

    def shifted(k, block, name):
        with jax.named_scope(name):
            return at.far_z[k % nz].shift(block)

    shards = jnp.stack([(at.z - jz) % nz * ny + (at.y - jy) % ny for jz, jy in order])
    shards = shards.astype(jnp.int32)
    forward_tables = [jnp.concatenate([mine[jx : jx + 1], swapped]) for jx in range(nx)]
    hidden_table = jnp.concatenate([quarters, shards])
    hiddens = both(hidden_rows, "hidden_core")
    first = [gathered(at.ring_1, grad_out, "own_first")]
    tables = jnp.concatenate([routing.astype(F32).T, gates.T])[None]
    plane = [grad_out]
    while len(tables) < nz:
        more = shifted(len(tables), tables[: nz - len(tables)], "routes_z")
        tables = jnp.concatenate([tables, more])
        if len(plane) == 1:
            tables = tie(tables, first[0], forward_tables, hidden_table, mine, theirs)
            plane.append(shifted(1, tie(grad_out, tables), "plane_1"))
            weights = both(tie(weight, tables, hiddens), "weight_core")
    first[0] = jnp.stack(first[0])
    second = [gathered(at.ring_2, first[0], "own_second")]
    tables = tie(gathered(at.ring_y, tables, "routes_y"), plane[1])
    plane.append(shifted(1, plane[1], "plane_2"))
    first.append(gathered(at.ring_1, plane[1], "plane_1_first"))
    backward_z = shifted(nz - 1, tie(grad_out, plane[1]), "plane_3")
    packed = jnp.stack([tables[jy][jz] for jz, jy in order])

    expert = lax.axis_index("expert")
    ours = [expert, expert - at.core + 1 - at.core] if two else [expert]
    ours = jnp.stack(ours).astype(F32)[:, None, None, None]
    hits = packed[None, :, :top] == ours
    hit = hits.astype(F32).sum(axis=2)
    gate = jnp.where(hits, packed[None, :, top:], 0.0).sum(axis=2)
    earlier = (jnp.arange(rows)[:, None] < jnp.arange(rows)[None, :]).astype(BF16)
    place = jnp.dot(hit.astype(BF16), earlier, preferred_element_type=F32).astype(jnp.int32)
    slot_of = jnp.where(hit > 0, place, -1)
    rows_in, turned = token_rows(slot_of, gate, hiddens, tie(shards, first[0]))
    slot_of, gate = slot_of[0], gate[0]

    calls = [(0, 0, 2), (0, 1, 2)] + [(jx, 0, 1) for jx in range(1, nx)]

    def forward(call, placed, *after):
        jx, part, parts = call
        table = tie(forward_tables[jx], *after)
        return forward_placed(rows_in, weights, table, jx, part, parts, places, size, at, placed)

    def assembled(blocks):
        plan = []
        for i in range(len(blocks) // nx):
            for j2 in range(nx):
                for j1 in range(ny):
                    number = i * nx + j2
                    plan.append((number, j1, (j1, j2), i * rows, size, blocks[number].shape[1]))
        return list(put_together(plan, blocks, swapped, nx, (half, width)))

    first[1] = jnp.stack(tie(first[1], rows_in))
    second.append(gathered(at.ring_2, first[1], "plane_1_second"))
    done = forward(calls[0], None, first[1], second[0])
    plane[2], plane_3 = tie((plane[2], backward_z), done)
    pair = jnp.stack([plane[2], plane_3])
    first.append(gathered(at.ring_1, pair, "pair_first"))
    done = forward(calls[1], done, pair)
    first[2] = jnp.stack(tie(first[2], done)).reshape(ny, size, width)
    second.append(gathered(at.ring_2, first[2], "pair_second"))
    grads_1 = assembled(tie(second[0] + second[1], done))
    others_1 = [both(block, "gradients_core")[-1] for block in grads_1] if two else []
    placed = done
    for call in calls[2:]:
        placed = forward(call, placed, first[2], grads_1)

    class Sum:
        def __init__(self, turn):
            self.name = "sum_%d" % turn
            self.terms = list(placed[turn * nx : (turn + 1) * nx])

        def start(self, ring, after=()):
            with jax.named_scope(self.name):
                self.terms = tie(self.terms, after)
                total = self.terms[1]
                for j in range(2, ring.size):
                    total = self.terms[j] + ring.shift(total)
                self.sent = total
                self.got = ring.shift(total)

        def finish(self, after):
            self.terms = self.terms[0] + tie(self.got, after)

        def second(self):
            self.terms = [self.terms[j] for j in range(ny)]
            self.start(at.ring_1)

    near, far = Sum(0), Sum(1)
    far.start(at.ring_2)
    ask = tie(hidden_table, far.sent)
    count = len(order) // 2
    back = hidden_gradient(gate[:count], slot_of[:count], grads_1 + others_1, weight, ask, capacity)

    grads_2 = assembled(tie(second[2], back))
    others_2 = [both(block, "gradients_core")[-1] for block in grads_2] if two else []
    ask = tie(mine, grads_2)
    grad_weight = weight_gradient(turned, list(zip(grads_1, grads_2)), ask, weight.shape, None)
    far.finish(grad_weight)
    far.second()
    near.start(at.ring_2)
    ask = tie(theirs, far.sent, near.sent)
    if two:
        grad_weight = weight_gradient(
            turned, list(zip(others_1, others_2)), ask, weight.shape, grad_weight
        )
    far.finish(grad_weight)
    near.finish(grad_weight)
    near.second()
    last = shifted(nz - 3, far.terms[rows:], "sum_3_z")
    onward = shifted(nz - 1, far.terms[:rows], "sum_2_z")
    ask = tie(hidden_table, far.terms, near.sent)
    grad_hidden = hidden_gradient(
        gate[count:],
        slot_of[count:],
        grads_2 + others_2,
        weight,
        ask,
        capacity,
        back,
    )
    near.finish(grad_hidden)
    onward = tie(onward, grad_hidden) + near.terms[rows:]
    onward = shifted(nz - 1, onward, "sum_1_z")
    mixed_out = near.terms[:rows].astype(F32) + last.astype(F32) + onward.astype(F32)
    return (mixed_out.astype(BF16), grad_hidden[None], grad_weight[None])


def solution(mesh):
    return jax.shard_map(
        body,
        mesh=mesh,
        in_specs=(
            P("expert", None, "dp"),
            P("expert", "dp", None),
            P("dp", "expert"),
            P("dp", None),
            P("dp", None),
        ),
        out_specs=(P("dp", "expert"), P("expert", None, "dp"), P("expert", "dp", None)),
        check_vma=False,
    )
```

```python
import functools
import jax
import jax.numpy as jnp
from jax import lax
from jax.experimental import pallas as pl
from jax.experimental.pallas import tpu as pltpu
from jax.sharding import PartitionSpec as P

BF16, F32 = jnp.bfloat16, jnp.float32
ALL = ("dp", "expert")
VMEM = 44 * 2**20


def cost(flops, moved):
    return pl.CostEstimate(flops=flops, bytes_accessed=moved, transcendentals=0)


class Ring:
    def __init__(self, size, perm):
        self.size, self.perm = size, perm

    def shift(self, block):
        return lax.ppermute(block, ALL, self.perm)

    def gather(self, block):
        blocks = [block]
        for _ in range(self.size - 1):
            blocks.append(self.shift(blocks[-1]))
        return blocks

    def scatter(self, blocks):
        if self.size == 1:
            return blocks[0]
        total = blocks[1]
        for j in list(range(2, self.size)) + [0]:
            total = blocks[j] + self.shift(total)
        return total


class Layout:
    def __init__(self):
        self.groups, self.owners = lax.axis_size("dp"), lax.axis_size("expert")
        self.nc = 2 if self.owners % 2 == 0 else 1
        self.nx = self.owners // self.nc
        self.ny = self.nx if self.groups % self.nx == 0 else 1
        self.nz = self.groups // self.ny
        dp, expert = lax.axis_index("dp"), lax.axis_index("expert")
        self.z, self.y = dp // self.ny, dp % self.ny
        self.x, self.core = expert // self.nc, expert % self.nc
        self.mixed = self.nx == self.ny and self.nc == 2
        step = {
            "x": lambda z, y, x, c: (z, y, (x + 1) % self.nx, c),
            "y": lambda z, y, x, c: (z, (y + 1) % self.ny, x, c),
            "c": lambda z, y, x, c: (z, y, x, (c + 1) % self.nc),
        }
        swapped = lambda c: self.mixed and c == 1
        self.far_z = [
            self.ring(self.nz, lambda z, y, x, c, k=k: ((z + k) % self.nz, y, x, c))
            for k in range(self.nz)
        ]
        self.ring_y = self.ring(self.ny, step["y"])
        self.ring_c = self.ring(self.nc, step["c"])
        self.ring_1 = self.ring(
            self.ny, lambda z, y, x, c: step["x" if swapped(c) else "y"](z, y, x, c)
        )
        self.ring_2 = self.ring(
            self.nx, lambda z, y, x, c: step["y" if swapped(c) else "x"](z, y, x, c)
        )

    def ring(self, size, onward):
        flat = lambda z, y, x, c: ((z * self.ny + y) * self.nx + x) * self.nc + c
        perm = []
        for z in range(self.nz):
            for y in range(self.ny):
                for x in range(self.nx):
                    for c in range(self.nc):
                        perm.append((flat(z, y, x, c), flat(*onward(z, y, x, c))))
        return Ring(size, perm)


def tile_of(width, most):
    tile = most
    while width % tile:
        tile -= 128
    return tile


def rows_kernel(size, shards, slots, gates, *rest):
    hidden, (out, turned) = rest[:-2], rest[-2:]
    count = shards.shape[0]
    capacity = hidden[0].shape[0] // count
    numbers = lax.broadcasted_iota(jnp.int32, (size, capacity), 1)
    for e, source in enumerate(hidden):
        slot_columns, gate_columns = slots[e].T, gates[e].T
        for i in range(count):
            block = source[pl.ds(pl.multiple_of(shards[i] * capacity, capacity), capacity), :]
            chosen = (slot_columns[:, i : i + 1] == numbers).astype(F32).astype(BF16)
            picked = jnp.dot(chosen, block, preferred_element_type=F32)
            picked = (picked * gate_columns[:, i : i + 1]).astype(BF16)
            out[e, pl.ds(i * size, size), :] = picked
            if e == 0:
                turned[:, pl.ds(i * size, size)] = picked.T


def token_rows(slot_of, gates, hidden, shards):
    experts, count, size = gates.shape
    tokens = count * size
    slots, depth = hidden[0].shape
    tile = tile_of(depth, 512)
    narrow = pl.BlockSpec((experts, count, size), lambda j, t: (0, 0, 0))
    return pl.pallas_call(
        functools.partial(rows_kernel, size),
        grid_spec=pltpu.PrefetchScalarGridSpec(
            num_scalar_prefetch=1,
            grid=(depth // tile,),
            in_specs=[narrow, narrow]
            + [pl.BlockSpec((slots, tile), lambda j, t: (0, j)) for _ in hidden],
            out_specs=[
                pl.BlockSpec((experts, tokens, tile), lambda j, t: (0, 0, j)),
                pl.BlockSpec((tile, tokens), lambda j, t: (j, 0)),
            ],
        ),
        out_shape=[
            jax.ShapeDtypeStruct((experts, tokens, depth), BF16),
            jax.ShapeDtypeStruct((depth, tokens), BF16),
        ],
        compiler_params=pltpu.CompilerParams(vmem_limit_bytes=VMEM),
        cost_estimate=cost(2 * tokens * slots * depth, 4 * experts * tokens * depth),
        name="token_rows",
    )(shards, slot_of, gates, *hidden)


def place_kernel(jx, first_tile, ny, plan, mixed, experts, table, rows, *rest):
    weights = rest[:experts]
    stage, sems = rest[-2:]
    outs = rest[-2 - sum(len(group[3]) for group in plan) : -2]
    step, steps = pl.program_id(0), pl.num_programs(0)
    tile = weights[0].shape[1]
    acc = jnp.dot(rows[0], weights[0][...], preferred_element_type=F32)
    for e in range(1, experts):
        acc = acc + jnp.dot(rows[e], weights[e][...], preferred_element_type=F32)
    stage[step] = acc.astype(BF16)

    def copies(at, act):
        columns = pl.ds(pl.multiple_of((first_tile + at) * tile, 128), tile)
        for g, (first, stride, size, numbers) in enumerate(plan):
            for jy in range(ny):

                def copy(k1, k2, first=first + jy * stride, size=size, numbers=numbers, g=g, jy=jy):
                    act(
                        pltpu.make_async_copy(
                            stage.at[at, pl.ds(first, size), :],
                            outs[numbers[k1]].at[k2, :, columns],
                            sems.at[at, g * ny + jy],
                        )
                    )

                if not mixed or jx == jy:
                    copy(jx, jy)
                else:
                    pl.when(table[1] == 0)(functools.partial(copy, jx, jy))
                    pl.when(table[1] != 0)(functools.partial(copy, jy, jx))

    copies(step, lambda copy: copy.start())

    @pl.when(step == steps - 1)
    def _():
        for at in range(stage.shape[0]):
            copies(at, lambda copy: copy.wait())


def forward_placed(rows, weights, table, jx, part, parts, places, at, before):
    experts, tokens, depth = rows.shape
    width = weights[0].shape[1] // at.owners
    tile = tile_of(width // parts, 384)
    per = width // parts // tile
    plan, shapes = [], []
    for first, stride, size in places:
        plan.append((first, stride, size, [len(shapes) + k for k in range(at.nx)]))
        shapes += [jax.ShapeDtypeStruct((at.ny, size, width), BF16)] * at.nx
    block = pl.BlockSpec((depth, tile), lambda j, t: (0, (t[0] * parts + part) * per + j))
    specs = [pl.BlockSpec((experts, tokens, depth), lambda j, t: (0, 0, 0))] + [block] * experts
    operands = [rows] + list(weights)
    aliases = {}
    if before is not None:
        aliases = {1 + len(operands) + i: i for i in range(len(shapes))}
        specs += [pl.BlockSpec(memory_space=pltpu.HBM)] * len(shapes)
        operands += list(before)
    return pl.pallas_call(
        functools.partial(place_kernel, jx, part * per, at.ny, plan, at.mixed, experts),
        grid_spec=pltpu.PrefetchScalarGridSpec(
            num_scalar_prefetch=1,
            grid=(per,),
            in_specs=specs,
            out_specs=[pl.BlockSpec(memory_space=pltpu.HBM)] * len(shapes),
            scratch_shapes=[
                pltpu.VMEM((per, tokens, tile), BF16),
                pltpu.SemaphoreType.DMA((per, len(places) * at.ny)),
            ],
        ),
        out_shape=shapes,
        input_output_aliases=aliases,
        compiler_params=pltpu.CompilerParams(vmem_limit_bytes=VMEM),
        cost_estimate=cost(
            2 * experts * tokens * depth * tile * per, 2 * tile * per * (2 * depth + 2 * tokens)
        ),
        name="forward_placed",
    )(table, *operands)


def gather_kernel(plan, outputs, swapped, *rest):
    sources = max(item[0] for item in plan) + 1
    blocks, outs, (stage, loads, stores) = rest[:sources], rest[-3 - outputs : -3], rest[-3:]
    places, done = [], 0
    for i, (number, index, _, _, _, size) in enumerate(plan):
        places.append(stage.at[pl.ds(done, size)])
        done += size
        pltpu.make_async_copy(blocks[number].at[index], places[i], loads.at[i]).start()

    def store(i, act):
        _, _, (j1, j2), first, stride, size = plan[i]

        def copy(jy, jx):
            target = outs[jx].at[pl.ds(first + jy * stride, size)]
            act(pltpu.make_async_copy(places[i], target, stores.at[i]))

        if j1 == j2:
            copy(j1, j2)
        else:
            pl.when(swapped[0] == 0)(functools.partial(copy, j1, j2))
            if max(j1, j2) < outputs:
                pl.when(swapped[0] != 0)(functools.partial(copy, j2, j1))

    for i, (number, index, _, _, _, size) in enumerate(plan):
        pltpu.make_async_copy(blocks[number].at[index], places[i], loads.at[i]).wait()
        store(i, lambda copy: copy.start())
    for i in range(len(plan)):
        store(i, lambda copy: copy.wait())


def put_together(plan, blocks, swapped, count, shape):
    return pl.pallas_call(
        functools.partial(gather_kernel, plan, count),
        grid_spec=pltpu.PrefetchScalarGridSpec(
            num_scalar_prefetch=1,
            grid=(1,),
            in_specs=[pl.BlockSpec(memory_space=pl.ANY)] * len(blocks),
            out_specs=[pl.BlockSpec(memory_space=pltpu.HBM)] * count,
            scratch_shapes=[
                pltpu.VMEM((sum(item[5] for item in plan), shape[-1]), BF16),
                pltpu.SemaphoreType.DMA((len(plan),)),
                pltpu.SemaphoreType.DMA((len(plan),)),
            ],
        ),
        out_shape=[jax.ShapeDtypeStruct(shape, BF16)] * count,
        compiler_params=pltpu.CompilerParams(vmem_limit_bytes=VMEM),
        cost_estimate=cost(0, 4 * sum(b.size for b in blocks)),
        name="put_together",
    )(swapped, *blocks)


def weight_kernel(count, per, quarters, turned, *rest):
    sources = (len(rest) - 1) // count
    step = pl.program_id(0)
    for i in range(count):

        @pl.when(step // per == i)
        def _(i=i):
            total, first = None, 0
            for block in rest[i * sources : (i + 1) * sources]:
                size = block.shape[0]
                part = jnp.dot(
                    turned[:, first : first + size], block[...], preferred_element_type=F32
                )
                total = part if total is None else total + part
                first += size
            rest[-1][...] = total.astype(BF16)


def weight_gradient(turned, grads, quarters, shape, before):
    depth, tokens = turned.shape
    count = len(grads)
    width = grads[0][0].shape[1]
    tile = tile_of(width, 768)
    per = width // tile
    specs = [pl.BlockSpec((depth, tokens), lambda j, q: (0, 0))]
    operands = [turned]
    for i in range(count):
        for block in grads[i]:
            specs.append(
                pl.BlockSpec(
                    (block.shape[0], tile), lambda j, q, i=i: (0, jnp.clip(j - i * per, 0, per - 1))
                )
            )
            operands.append(block)
    aliases, extra = {}, []
    kernel = functools.partial(weight_kernel, count, per)
    if before is not None:
        specs.append(pl.BlockSpec(memory_space=pltpu.HBM))
        aliases = {len(operands) + 1: 0}
        operands.append(before)
        inner = kernel
        kernel = lambda quarters, turned, *rest: inner(quarters, turned, *rest[:-2], rest[-1])
    return pl.pallas_call(
        kernel,
        grid_spec=pltpu.PrefetchScalarGridSpec(
            num_scalar_prefetch=1,
            grid=(count * per,),
            in_specs=specs,
            out_specs=pl.BlockSpec((depth, tile), lambda j, q: (0, q[j // per] * per + j % per)),
        ),
        out_shape=jax.ShapeDtypeStruct(shape, BF16),
        input_output_aliases=aliases,
        compiler_params=pltpu.CompilerParams(vmem_limit_bytes=VMEM),
        cost_estimate=cost(
            2 * tokens * depth * width * count, 2 * count * width * (depth + tokens)
        ),
        name="weight_gradient",
    )(quarters, *operands)


def hidden_kernel(steps, each, count, last, table, gates, slots, weight, *rest):
    out, total = rest[-2:]
    sources = steps // each
    step = pl.program_id(0)
    size = total.shape[0] // count

    @pl.when(step == 0)
    def _():
        total[...] = jnp.zeros_like(total)

    for i, block in enumerate(rest[:sources]):

        @pl.when(step // each == i)
        def _(block=block):
            total[...] += lax.dot_general(
                block[...], weight[...], (((1,), (1,)), ((), ())), preferred_element_type=F32
            )

    @pl.when(step == steps - 1)
    def _():
        capacity = out.shape[0] // (2 * count if last else count)
        numbers = lax.broadcasted_iota(jnp.int32, (capacity, size), 0)
        gate_columns = gates[...].T
        for i in range(count):
            span = pl.ds(i * size, size)
            back = (total[span, :] * gate_columns[:, i : i + 1]).astype(BF16)
            chosen = (slots[pl.ds(i, 1), :] == numbers).astype(F32).astype(BF16)
            picked = jnp.dot(chosen, back, preferred_element_type=F32).astype(BF16)
            if last:
                before = rest[sources]
                place = table[steps // each + count + i] * capacity
                out[pl.ds(pl.multiple_of(place, capacity), capacity), :] = picked
                place = table[steps // each + i] * capacity
                old = before[pl.ds(i * capacity, capacity), :]
                out[pl.ds(pl.multiple_of(place, capacity), capacity), :] = old
            else:
                out[pl.ds(i * capacity, capacity), :] = picked


def hidden_gradient(gates, slots, grads, weight, table, capacity, before=None):
    tokens, width = grads[0].shape
    depth = weight.shape[0]
    tile = tile_of(width, 1536)
    per = width // tile
    steps = per * len(grads)
    last = before is not None
    number = slots.shape[0]
    height = capacity * number * (2 if last else 1)
    specs = [
        pl.BlockSpec(gates.shape, lambda s, t: (0, 0)),
        pl.BlockSpec(slots.shape, lambda s, t: (0, 0)),
        pl.BlockSpec((depth, tile), lambda s, t: (0, t[s // per] * per + s % per)),
    ]
    for i in range(len(grads)):

        def place(s, t, i=i):
            return (0, jnp.clip(s - i * per, 0, per - 1))

        specs.append(pl.BlockSpec((tokens, tile), place))
    operands = [gates, slots, weight] + list(grads)
    if last:
        specs.append(pl.BlockSpec(before.shape, lambda s, t: (0, 0)))
        operands.append(before)
    return pl.pallas_call(
        functools.partial(hidden_kernel, steps, per, number, last),
        grid_spec=pltpu.PrefetchScalarGridSpec(
            num_scalar_prefetch=1,
            grid=(steps,),
            in_specs=specs,
            out_specs=pl.BlockSpec((height, depth), lambda s, t: (0, 0)),
            scratch_shapes=[pltpu.VMEM((tokens, depth), F32)],
        ),
        out_shape=jax.ShapeDtypeStruct((height, depth), BF16),
        compiler_params=pltpu.CompilerParams(vmem_limit_bytes=VMEM),
        cost_estimate=cost(2 * steps * tile * tokens * depth, 2 * steps * tile * (depth + tokens)),
        name="hidden_gradient",
    )(table, *operands)


def tie(value, *others):
    return lax.optimization_barrier((value, others))[0]


def body(hidden, down_weight, grad_out, routing, gates):
    at = Layout()
    nx, ny, nz = at.nx, at.ny, at.nz
    rows, width = grad_out.shape
    top = routing.shape[1]
    slots = hidden.shape[1]
    capacity = slots // at.groups
    hidden_rows, weight = hidden[0], down_weight[0]

    turns = [list(range(nz // 2)), list(range(nz // 2, nz))]
    order = [(jz, jy) for turn in turns for jy in range(ny) for jz in turn]
    size = len(turns[0]) * rows
    half = ny * size
    places = [(i * rows, size, rows) for i in range(len(turns[0]))] + [(half, size, size)]
    swapped = ((at.core == 1) if at.mixed else (at.core < 0)).astype(jnp.int32)[None]
    back_x = (at.x - jnp.arange(nx)) % nx * at.nc
    mine = (back_x + at.core).astype(jnp.int32)
    theirs = (back_x + (at.core + at.nc - 1) % at.nc).astype(jnp.int32)
    two = at.nc > 1
    quarters = jnp.concatenate([mine, theirs]) if two else mine

    def both(block, name):
        with jax.named_scope(name):
            return [block, at.ring_c.shift(block)] if two else [block]

    def gathered(ring, block, name):
        with jax.named_scope(name):
            return ring.gather(block)

    def shifted(k, block, name):
        with jax.named_scope(name):
            return at.far_z[k % nz].shift(block)

    shards = jnp.stack([(at.z - jz) % nz * ny + (at.y - jy) % ny for jz, jy in order])
    shards = shards.astype(jnp.int32)
    forward_tables = [jnp.concatenate([mine[jx : jx + 1], swapped]) for jx in range(nx)]
    hidden_table = jnp.concatenate([quarters, shards])
    hiddens = both(hidden_rows, "hidden_core")
    first = [gathered(at.ring_1, grad_out, "own_first")]
    tables = jnp.concatenate([routing.astype(F32).T, gates.T])[None]
    plane = [grad_out]
    while len(tables) < nz:
        more = shifted(len(tables), tables[: nz - len(tables)], "routes_z")
        tables = jnp.concatenate([tables, more])
        if len(plane) == 1:
            tables = tie(tables, first[0], forward_tables, hidden_table, mine, theirs)
            plane.append(shifted(1, tie(grad_out, tables), "plane_1"))
            weights = both(tie(weight, tables, hiddens), "weight_core")
    first[0] = jnp.stack(first[0])
    second = [gathered(at.ring_2, first[0], "own_second")]
    tables = gathered(at.ring_y, tables, "routes_y")
    packed = jnp.stack([tables[jy][jz] for jz, jy in order])

    expert = lax.axis_index("expert")
    ours = [expert, expert - at.core + 1 - at.core] if two else [expert]
    ours = jnp.stack(ours).astype(F32)[:, None, None, None]
    hits = packed[None, :, :top] == ours
    hit = hits.astype(F32).sum(axis=2)
    gate = jnp.where(hits, packed[None, :, top:], 0.0).sum(axis=2)
    earlier = (jnp.arange(rows)[:, None] < jnp.arange(rows)[None, :]).astype(BF16)
    place = jnp.dot(hit.astype(BF16), earlier, preferred_element_type=F32).astype(jnp.int32)
    slot_of = jnp.where(hit > 0, place, -1)
    rows_in, turned = token_rows(slot_of, gate, hiddens, tie(shards, first[0]))
    slot_of, gate = slot_of[0], gate[0]

    calls = [(jx, part, 2) for jx in range(nx) for part in range(2)]

    def forward(call, placed, *after):
        jx, part, parts = call
        table = tie(forward_tables[jx], *after)
        return forward_placed(rows_in, weights, table, jx, part, parts, places, at, placed)

    def assembled(blocks):
        plan = []
        for i in range(len(blocks) // nx):
            for j2 in range(nx):
                for j1 in range(ny):
                    number = i * nx + j2
                    plan.append((number, j1, (j1, j2), i * rows, size, blocks[number].shape[1]))
        return list(put_together(plan, blocks, swapped, nx, (half, width)))

    plane[1] = tie(plane[1], rows_in)
    plane.append(shifted(1, plane[1], "plane_2"))
    plane.append(shifted(nz - 1, tie(grad_out, plane[1]), "plane_3"))
    first.append(gathered(at.ring_1, plane[1], "plane_1_first"))
    done = forward(calls[0], None, plane[1])
    first[1] = jnp.stack(tie(first[1], done))
    second.append(gathered(at.ring_2, first[1], "plane_1_second"))
    done = forward(calls[1], done, first[1], second[0])
    pair = jnp.stack(tie(plane[2:], done))
    first.append(gathered(at.ring_1, pair, "pair_first"))
    for call in calls[2:-1]:
        done = forward(call, done, pair)
    first[2] = jnp.stack(tie(first[2], done)).reshape(ny, size, width)
    second.append(gathered(at.ring_2, first[2], "pair_second"))
    grads_1 = assembled(tie(second[0] + second[1], done))
    others_1 = [both(block, "gradients_core")[-1] for block in grads_1] if two else []
    placed = forward(calls[-1], done, first[2], grads_1)

    class Sum:
        def __init__(self, turn):
            self.name = "sum_%d" % turn
            self.terms = list(placed[turn * nx : (turn + 1) * nx])

        def start(self, ring, after=()):
            with jax.named_scope(self.name):
                self.terms = tie(self.terms, after)
                total = self.terms[1]
                for j in range(2, ring.size):
                    total = self.terms[j] + ring.shift(total)
                self.sent = total
                self.got = ring.shift(total)

        def finish(self, after):
            self.terms = self.terms[0] + tie(self.got, after)

        def second(self):
            self.terms = [self.terms[j] for j in range(ny)]
            self.start(at.ring_1)

    own_sum, next_sum, far = [Sum(i) for i in range(len(places))]
    far.start(at.ring_2)
    ask = tie(hidden_table, far.sent)
    count = len(order) // 2
    back = hidden_gradient(gate[:count], slot_of[:count], grads_1 + others_1, weight, ask, capacity)

    grads_2 = assembled(tie(second[2], back))
    others_2 = [both(block, "gradients_core")[-1] for block in grads_2] if two else []
    next_sum.start(at.ring_2, back)
    pairs = list(zip(grads_1, grads_2))
    ask = tie(mine, grads_2, next_sum.sent)
    grad_weight = weight_gradient(turned, pairs, ask, weight.shape, None)
    far.finish(grad_weight)
    far.second()
    if two:
        pairs = list(zip(others_1, others_2))
        ask = tie(theirs, far.sent)
        grad_weight = weight_gradient(turned, pairs, ask, weight.shape, grad_weight)
    own_sum.start(at.ring_2, grad_weight)
    next_sum.finish(grad_weight)
    far.finish((grad_weight, next_sum.terms))
    next_sum.second()
    last = shifted(nz - 3, far.terms[rows:], "sum_3_z")
    onward = shifted(nz - 1, far.terms[:rows], "sum_2_z")
    ask = tie(hidden_table, own_sum.sent, next_sum.sent, far.terms)
    grad_hidden = hidden_gradient(
        gate[count:],
        slot_of[count:],
        grads_2 + others_2,
        weight,
        ask,
        capacity,
        back,
    )
    own_sum.finish(grad_hidden)
    own_sum.second()
    next_sum.finish(grad_hidden)
    onward, last = tie((onward, last), grad_hidden)
    onward = tie(onward, last) + next_sum.terms
    onward = shifted(nz - 1, onward, "sum_1_z")
    own_sum.finish(grad_hidden)
    mixed_out = own_sum.terms.astype(F32) + last.astype(F32) + onward.astype(F32)
    return (mixed_out.astype(BF16), grad_hidden[None], grad_weight[None])


def solution(mesh):
    return jax.shard_map(
        body,
        mesh=mesh,
        in_specs=(
            P("expert", None, "dp"),
            P("expert", "dp", None),
            P("dp", "expert"),
            P("dp", None),
            P("dp", None),
        ),
        out_specs=(P("dp", "expert"), P("expert", None, "dp"), P("expert", "dp", None)),
        check_vma=False,
    )
```

```python
import functools
import jax
import jax.numpy as jnp
from jax import lax
from jax.experimental import pallas as pl
from jax.experimental.pallas import tpu as pltpu
from jax.sharding import PartitionSpec as P

BF16, F32 = jnp.bfloat16, jnp.float32
ALL = ("dp", "expert")
VMEM = 36 * 2**20


def cost(flops, moved):
    return pl.CostEstimate(flops=flops, bytes_accessed=moved, transcendentals=0)


class Ring:
    def __init__(self, size, perm):
        self.size, self.perm = size, perm

    def shift(self, block):
        return lax.ppermute(block, ALL, self.perm)

    def gather(self, block):
        blocks = [block]
        for _ in range(self.size - 1):
            blocks.append(self.shift(blocks[-1]))
        return blocks

    def scatter(self, blocks):
        if self.size == 1:
            return blocks[0]
        total = blocks[1]
        for j in list(range(2, self.size)) + [0]:
            total = blocks[j] + self.shift(total)
        return total


class Layout:
    def __init__(self):
        self.groups, self.owners = lax.axis_size("dp"), lax.axis_size("expert")
        self.nc = 2 if self.owners % 2 == 0 else 1
        self.nx = self.owners // self.nc
        self.ny = self.nx if self.groups % self.nx == 0 else 1
        self.nz = self.groups // self.ny
        dp, expert = lax.axis_index("dp"), lax.axis_index("expert")
        self.z, self.y = dp // self.ny, dp % self.ny
        self.x, self.core = expert // self.nc, expert % self.nc
        self.mixed = self.nx == self.ny and self.nc == 2
        step = {
            "x": lambda z, y, x, c: (z, y, (x + 1) % self.nx, c),
            "y": lambda z, y, x, c: (z, (y + 1) % self.ny, x, c),
            "c": lambda z, y, x, c: (z, y, x, (c + 1) % self.nc),
        }
        swapped = lambda c: self.mixed and c == 1
        self.far_z = [
            self.ring(self.nz, lambda z, y, x, c, k=k: ((z + k) % self.nz, y, x, c))
            for k in range(self.nz)
        ]
        self.ring_y = self.ring(self.ny, step["y"])
        self.ring_c = self.ring(self.nc, step["c"])
        self.ring_1 = self.ring(
            self.ny, lambda z, y, x, c: step["x" if swapped(c) else "y"](z, y, x, c)
        )
        self.ring_2 = self.ring(
            self.nx, lambda z, y, x, c: step["y" if swapped(c) else "x"](z, y, x, c)
        )

    def ring(self, size, onward):
        flat = lambda z, y, x, c: ((z * self.ny + y) * self.nx + x) * self.nc + c
        perm = []
        for z in range(self.nz):
            for y in range(self.ny):
                for x in range(self.nx):
                    for c in range(self.nc):
                        perm.append((flat(z, y, x, c), flat(*onward(z, y, x, c))))
        return Ring(size, perm)


def tile_of(width, most):
    tile = most
    while width % tile:
        tile -= 128
    return tile


def rows_kernel(size, shards, slots, gates, *rest):
    hidden, (out, turned) = rest[:-2], rest[-2:]
    count = shards.shape[0]
    capacity = hidden[0].shape[0] // count
    numbers = lax.broadcasted_iota(jnp.int32, (size, capacity), 1)
    for e, source in enumerate(hidden):
        slot_columns, gate_columns = slots[e].T, gates[e].T
        for i in range(count):
            block = source[pl.ds(pl.multiple_of(shards[i] * capacity, capacity), capacity), :]
            chosen = (slot_columns[:, i : i + 1] == numbers).astype(F32).astype(BF16)
            picked = jnp.dot(chosen, block, preferred_element_type=F32)
            picked = (picked * gate_columns[:, i : i + 1]).astype(BF16)
            out[e, pl.ds(i * size, size), :] = picked
            if e == 0:
                turned[:, pl.ds(i * size, size)] = picked.T


def token_rows(slot_of, gates, hidden, shards):
    experts, count, size = gates.shape
    tokens = count * size
    slots, depth = hidden[0].shape
    tile = tile_of(depth, 512)
    narrow = pl.BlockSpec((experts, count, size), lambda j, t: (0, 0, 0))
    return pl.pallas_call(
        functools.partial(rows_kernel, size),
        grid_spec=pltpu.PrefetchScalarGridSpec(
            num_scalar_prefetch=1,
            grid=(depth // tile,),
            in_specs=[narrow, narrow]
            + [pl.BlockSpec((slots, tile), lambda j, t: (0, j)) for _ in hidden],
            out_specs=[
                pl.BlockSpec((experts, tokens, tile), lambda j, t: (0, 0, j)),
                pl.BlockSpec((tile, tokens), lambda j, t: (j, 0)),
            ],
        ),
        out_shape=[
            jax.ShapeDtypeStruct((experts, tokens, depth), BF16),
            jax.ShapeDtypeStruct((depth, tokens), BF16),
        ],
        compiler_params=pltpu.CompilerParams(vmem_limit_bytes=VMEM),
        cost_estimate=cost(2 * tokens * slots * depth, 4 * experts * tokens * depth),
        name="token_rows",
    )(shards, slot_of, gates, *hidden)


def place_kernel(jx, first_tile, ny, plan, mixed, experts, table, rows, *rest):
    weights = rest[:experts]
    stage, sems = rest[-2:]
    outs = rest[-2 - sum(len(group[3]) for group in plan) : -2]
    step, steps = pl.program_id(0), pl.num_programs(0)
    tile = weights[0].shape[1]
    acc = jnp.dot(rows[0], weights[0][...], preferred_element_type=F32)
    for e in range(1, experts):
        acc = acc + jnp.dot(rows[e], weights[e][...], preferred_element_type=F32)
    stage[step] = acc.astype(BF16)

    def copies(at, act):
        columns = pl.ds(pl.multiple_of((first_tile + at) * tile, 128), tile)
        for g, (first, stride, size, numbers) in enumerate(plan):
            for jy in range(ny):

                def copy(k1, k2, first=first + jy * stride, size=size, numbers=numbers, g=g, jy=jy):
                    act(
                        pltpu.make_async_copy(
                            stage.at[at, pl.ds(first, size), :],
                            outs[numbers[k1]].at[k2, :, columns],
                            sems.at[at, g * ny + jy],
                        )
                    )

                if not mixed or jx == jy:
                    copy(jx, jy)
                else:
                    pl.when(table[1] == 0)(functools.partial(copy, jx, jy))
                    pl.when(table[1] != 0)(functools.partial(copy, jy, jx))

    copies(step, lambda copy: copy.start())

    @pl.when(step == steps - 1)
    def _():
        for at in range(stage.shape[0]):
            copies(at, lambda copy: copy.wait())


def forward_placed(rows, weights, table, jx, part, parts, places, at, before):
    experts, tokens, depth = rows.shape
    width = weights[0].shape[1] // at.owners
    tile = tile_of(width // parts, 384)
    per = width // parts // tile
    plan, shapes = [], []
    for first, stride, size in places:
        plan.append((first, stride, size, [len(shapes) + k for k in range(at.nx)]))
        shapes += [jax.ShapeDtypeStruct((at.ny, size, width), BF16)] * at.nx
    block = pl.BlockSpec((depth, tile), lambda j, t: (0, (t[0] * parts + part) * per + j))
    specs = [pl.BlockSpec((experts, tokens, depth), lambda j, t: (0, 0, 0))] + [block] * experts
    operands = [rows] + list(weights)
    aliases = {}
    if before is not None:
        aliases = {1 + len(operands) + i: i for i in range(len(shapes))}
        specs += [pl.BlockSpec(memory_space=pltpu.HBM)] * len(shapes)
        operands += list(before)
    return pl.pallas_call(
        functools.partial(place_kernel, jx, part * per, at.ny, plan, at.mixed, experts),
        grid_spec=pltpu.PrefetchScalarGridSpec(
            num_scalar_prefetch=1,
            grid=(per,),
            in_specs=specs,
            out_specs=[pl.BlockSpec(memory_space=pltpu.HBM)] * len(shapes),
            scratch_shapes=[
                pltpu.VMEM((per, tokens, tile), BF16),
                pltpu.SemaphoreType.DMA((per, len(places) * at.ny)),
            ],
        ),
        out_shape=shapes,
        input_output_aliases=aliases,
        compiler_params=pltpu.CompilerParams(vmem_limit_bytes=VMEM),
        cost_estimate=cost(
            2 * experts * tokens * depth * tile * per, 2 * tile * per * (2 * depth + 2 * tokens)
        ),
        name="forward_placed",
    )(table, *operands)


def gather_kernel(plan, outputs, swapped, *rest):
    sources = max(item[0] for item in plan) + 1
    blocks, outs, (stage, loads, stores) = rest[:sources], rest[-3 - outputs : -3], rest[-3:]
    places, done = [], 0
    for i, (number, index, _, _, _, size) in enumerate(plan):
        places.append(stage.at[pl.ds(done, size)])
        done += size
        pltpu.make_async_copy(blocks[number].at[index], places[i], loads.at[i]).start()

    def store(i, act):
        _, _, (j1, j2), first, stride, size = plan[i]

        def copy(jy, jx):
            target = outs[jx].at[pl.ds(first + jy * stride, size)]
            act(pltpu.make_async_copy(places[i], target, stores.at[i]))

        if j1 == j2:
            copy(j1, j2)
        else:
            pl.when(swapped[0] == 0)(functools.partial(copy, j1, j2))
            if max(j1, j2) < outputs:
                pl.when(swapped[0] != 0)(functools.partial(copy, j2, j1))

    for i, (number, index, _, _, _, size) in enumerate(plan):
        pltpu.make_async_copy(blocks[number].at[index], places[i], loads.at[i]).wait()
        store(i, lambda copy: copy.start())
    for i in range(len(plan)):
        store(i, lambda copy: copy.wait())


def put_together(plan, blocks, swapped, count, shape):
    return pl.pallas_call(
        functools.partial(gather_kernel, plan, count),
        grid_spec=pltpu.PrefetchScalarGridSpec(
            num_scalar_prefetch=1,
            grid=(1,),
            in_specs=[pl.BlockSpec(memory_space=pl.ANY)] * len(blocks),
            out_specs=[pl.BlockSpec(memory_space=pltpu.HBM)] * count,
            scratch_shapes=[
                pltpu.VMEM((sum(item[5] for item in plan), shape[-1]), BF16),
                pltpu.SemaphoreType.DMA((len(plan),)),
                pltpu.SemaphoreType.DMA((len(plan),)),
            ],
        ),
        out_shape=[jax.ShapeDtypeStruct(shape, BF16)] * count,
        compiler_params=pltpu.CompilerParams(vmem_limit_bytes=VMEM),
        cost_estimate=cost(0, 4 * sum(b.size for b in blocks)),
        name="put_together",
    )(swapped, *blocks)


def weight_kernel(count, per, quarters, turned, *rest):
    sources = (len(rest) - 1) // count
    step = pl.program_id(0)
    for i in range(count):

        @pl.when(step // per == i)
        def _(i=i):
            total, first = None, 0
            for block in rest[i * sources : (i + 1) * sources]:
                size = block.shape[0]
                part = jnp.dot(
                    turned[:, first : first + size], block[...], preferred_element_type=F32
                )
                total = part if total is None else total + part
                first += size
            rest[-1][...] = total.astype(BF16)


def weight_gradient(turned, grads, quarters, shape, before):
    depth, tokens = turned.shape
    count = len(grads)
    width = grads[0][0].shape[1]
    tile = tile_of(width, 768)
    per = width // tile
    specs = [pl.BlockSpec((depth, tokens), lambda j, q: (0, 0))]
    operands = [turned]
    for i in range(count):
        for block in grads[i]:
            specs.append(
                pl.BlockSpec(
                    (block.shape[0], tile), lambda j, q, i=i: (0, jnp.clip(j - i * per, 0, per - 1))
                )
            )
            operands.append(block)
    aliases, extra = {}, []
    kernel = functools.partial(weight_kernel, count, per)
    if before is not None:
        specs.append(pl.BlockSpec(memory_space=pltpu.HBM))
        aliases = {len(operands) + 1: 0}
        operands.append(before)
        inner = kernel
        kernel = lambda quarters, turned, *rest: inner(quarters, turned, *rest[:-2], rest[-1])
    return pl.pallas_call(
        kernel,
        grid_spec=pltpu.PrefetchScalarGridSpec(
            num_scalar_prefetch=1,
            grid=(count * per,),
            in_specs=specs,
            out_specs=pl.BlockSpec((depth, tile), lambda j, q: (0, q[j // per] * per + j % per)),
        ),
        out_shape=jax.ShapeDtypeStruct(shape, BF16),
        input_output_aliases=aliases,
        compiler_params=pltpu.CompilerParams(vmem_limit_bytes=VMEM),
        cost_estimate=cost(
            2 * tokens * depth * width * count, 2 * count * width * (depth + tokens)
        ),
        name="weight_gradient",
    )(quarters, *operands)


def hidden_kernel(steps, each, count, last, table, gates, slots, weight, *rest):
    out, total = rest[-2:]
    sources = steps // each
    step = pl.program_id(0)
    size = total.shape[0] // count

    @pl.when(step == 0)
    def _():
        total[...] = jnp.zeros_like(total)

    for i, block in enumerate(rest[:sources]):

        @pl.when(step // each == i)
        def _(block=block):
            total[...] += lax.dot_general(
                block[...], weight[...], (((1,), (1,)), ((), ())), preferred_element_type=F32
            )

    @pl.when(step == steps - 1)
    def _():
        capacity = out.shape[0] // (2 * count if last else count)
        numbers = lax.broadcasted_iota(jnp.int32, (capacity, size), 0)
        gate_columns = gates[...].T
        for i in range(count):
            span = pl.ds(i * size, size)
            back = (total[span, :] * gate_columns[:, i : i + 1]).astype(BF16)
            chosen = (slots[pl.ds(i, 1), :] == numbers).astype(F32).astype(BF16)
            picked = jnp.dot(chosen, back, preferred_element_type=F32).astype(BF16)
            if last:
                before = rest[sources]
                place = table[steps // each + count + i] * capacity
                out[pl.ds(pl.multiple_of(place, capacity), capacity), :] = picked
                place = table[steps // each + i] * capacity
                old = before[pl.ds(i * capacity, capacity), :]
                out[pl.ds(pl.multiple_of(place, capacity), capacity), :] = old
            else:
                out[pl.ds(i * capacity, capacity), :] = picked


def hidden_gradient(gates, slots, grads, weight, table, capacity, before=None):
    tokens, width = grads[0].shape
    depth = weight.shape[0]
    tile = tile_of(width, 1536)
    per = width // tile
    steps = per * len(grads)
    last = before is not None
    number = slots.shape[0]
    height = capacity * number * (2 if last else 1)
    specs = [
        pl.BlockSpec(gates.shape, lambda s, t: (0, 0)),
        pl.BlockSpec(slots.shape, lambda s, t: (0, 0)),
        pl.BlockSpec((depth, tile), lambda s, t: (0, t[s // per] * per + s % per)),
    ]
    for i in range(len(grads)):

        def place(s, t, i=i):
            return (0, jnp.clip(s - i * per, 0, per - 1))

        specs.append(pl.BlockSpec((tokens, tile), place))
    operands = [gates, slots, weight] + list(grads)
    if last:
        specs.append(pl.BlockSpec(before.shape, lambda s, t: (0, 0)))
        operands.append(before)
    return pl.pallas_call(
        functools.partial(hidden_kernel, steps, per, number, last),
        grid_spec=pltpu.PrefetchScalarGridSpec(
            num_scalar_prefetch=1,
            grid=(steps,),
            in_specs=specs,
            out_specs=pl.BlockSpec((height, depth), lambda s, t: (0, 0)),
            scratch_shapes=[pltpu.VMEM((tokens, depth), F32)],
        ),
        out_shape=jax.ShapeDtypeStruct((height, depth), BF16),
        compiler_params=pltpu.CompilerParams(vmem_limit_bytes=VMEM),
        cost_estimate=cost(2 * steps * tile * tokens * depth, 2 * steps * tile * (depth + tokens)),
        name="hidden_gradient",
    )(table, *operands)


def tie(value, *others):
    return lax.optimization_barrier((value, others))[0]


def body(hidden, down_weight, grad_out, routing, gates):
    at = Layout()
    nx, ny, nz = at.nx, at.ny, at.nz
    rows, width = grad_out.shape
    top = routing.shape[1]
    slots = hidden.shape[1]
    capacity = slots // at.groups
    hidden_rows, weight = hidden[0], down_weight[0]

    turns = [list(range(nz // 2)), list(range(nz // 2, nz))]
    order = [(jz, jy) for turn in turns for jy in range(ny) for jz in turn]
    size = len(turns[0]) * rows
    half = ny * size
    places = [(i * rows, size, rows) for i in range(len(turns[0]))] + [(half, size, size)]
    swapped = ((at.core == 1) if at.mixed else (at.core < 0)).astype(jnp.int32)[None]
    back_x = (at.x - jnp.arange(nx)) % nx * at.nc
    mine = (back_x + at.core).astype(jnp.int32)
    theirs = (back_x + (at.core + at.nc - 1) % at.nc).astype(jnp.int32)
    two = at.nc > 1
    quarters = jnp.concatenate([mine, theirs]) if two else mine

    def both(block, name):
        with jax.named_scope(name):
            return [block, at.ring_c.shift(block)] if two else [block]

    def gathered(ring, block, name):
        with jax.named_scope(name):
            return ring.gather(block)

    def shifted(k, block, name):
        with jax.named_scope(name):
            return at.far_z[k % nz].shift(block)

    shards = jnp.stack([(at.z - jz) % nz * ny + (at.y - jy) % ny for jz, jy in order])
    shards = shards.astype(jnp.int32)
    forward_tables = [jnp.concatenate([mine[jx : jx + 1], swapped]) for jx in range(nx)]
    hidden_table = jnp.concatenate([quarters, shards])
    hiddens = both(hidden_rows, "hidden_core")
    first = [gathered(at.ring_1, grad_out, "own_first")]
    tables = jnp.concatenate([routing.astype(F32).T, gates.T])[None]
    plane = [grad_out]
    while len(tables) < nz:
        more = shifted(len(tables), tables[: nz - len(tables)], "routes_z")
        tables = jnp.concatenate([tables, more])
        if len(plane) == 1:
            tables = tie(tables, first[0], forward_tables, hidden_table, mine, theirs)
            plane.append(shifted(1, tie(grad_out, tables), "plane_1"))
            weights = both(tie(weight, tables, hiddens), "weight_core")
    first[0] = jnp.stack(first[0])
    second = [gathered(at.ring_2, first[0], "own_second")]
    tables = gathered(at.ring_y, tables, "routes_y")
    packed = jnp.stack([tables[jy][jz] for jz, jy in order])

    expert = lax.axis_index("expert")
    ours = [expert, expert - at.core + 1 - at.core] if two else [expert]
    ours = jnp.stack(ours).astype(F32)[:, None, None, None]
    hits = packed[None, :, :top] == ours
    hit = hits.astype(F32).sum(axis=2)
    gate = jnp.where(hits, packed[None, :, top:], 0.0).sum(axis=2)
    earlier = (jnp.arange(rows)[:, None] < jnp.arange(rows)[None, :]).astype(BF16)
    place = jnp.dot(hit.astype(BF16), earlier, preferred_element_type=F32).astype(jnp.int32)
    slot_of = jnp.where(hit > 0, place, -1)
    rows_in, turned = token_rows(slot_of, gate, hiddens, tie(shards, first[0]))
    slot_of, gate = slot_of[0], gate[0]

    calls = [(jx, part, 2) for jx in range(nx) for part in range(2)]

    def forward(call, placed, *after):
        jx, part, parts = call
        table = tie(forward_tables[jx], *after)
        return forward_placed(rows_in, weights, table, jx, part, parts, places, at, placed)

    def assembled(blocks):
        plan = []
        for i in range(len(blocks) // nx):
            for j2 in range(nx):
                for j1 in range(ny):
                    number = i * nx + j2
                    plan.append((number, j1, (j1, j2), i * rows, size, blocks[number].shape[1]))
        return list(put_together(plan, blocks, swapped, nx, (half, width)))

    plane[1] = tie(plane[1], rows_in)
    plane.append(shifted(1, plane[1], "plane_2"))
    plane.append(shifted(nz - 1, tie(grad_out, plane[1]), "plane_3"))
    first.append(gathered(at.ring_1, plane[1], "plane_1_first"))
    done = forward(calls[0], None, plane[1])
    first[1] = jnp.stack(tie(first[1], done))
    second.append(gathered(at.ring_2, first[1], "plane_1_second"))
    done = forward(calls[1], done, first[1], second[0])
    pair = jnp.stack(tie(plane[2:], done))
    first.append(gathered(at.ring_1, pair, "pair_first"))
    for call in calls[2:-1]:
        done = forward(call, done, pair)
    first[2] = jnp.stack(tie(first[2], done)).reshape(ny, size, width)
    second.append(gathered(at.ring_2, first[2], "pair_second"))
    grads_1 = assembled(tie(second[0] + second[1], done))
    others_1 = [both(block, "gradients_core")[-1] for block in grads_1] if two else []
    placed = forward(calls[-1], done, first[2], grads_1)

    class Sum:
        def __init__(self, turn):
            self.name = "sum_%d" % turn
            self.terms = list(placed[turn * nx : (turn + 1) * nx])

        def start(self, ring, after=()):
            with jax.named_scope(self.name):
                self.terms = tie(self.terms, after)
                total = self.terms[1]
                for j in range(2, ring.size):
                    total = self.terms[j] + ring.shift(total)
                self.sent = total
                self.got = ring.shift(total)

        def finish(self, after):
            self.terms = self.terms[0] + tie(self.got, after)

        def second(self):
            self.terms = [self.terms[j] for j in range(ny)]
            self.start(at.ring_1)

    own_sum, next_sum, far = [Sum(i) for i in range(len(places))]
    far.start(at.ring_2)
    ask = tie(hidden_table, far.sent)
    count = len(order) // 2
    back = hidden_gradient(gate[:count], slot_of[:count], grads_1 + others_1, weight, ask, capacity)

    grads_2 = assembled(tie(second[2], back))
    others_2 = [both(block, "gradients_core")[-1] for block in grads_2] if two else []
    next_sum.start(at.ring_2, back)
    pairs = list(zip(grads_1, grads_2))
    ask = tie(mine, grads_2, next_sum.sent)
    grad_weight = weight_gradient(turned, pairs, ask, weight.shape, None)
    far.finish(grad_weight)
    far.second()
    if two:
        pairs = list(zip(others_1, others_2))
        ask = tie(theirs, far.sent)
        grad_weight = weight_gradient(turned, pairs, ask, weight.shape, grad_weight)
    own_sum.start(at.ring_2, grad_weight)
    next_sum.finish(grad_weight)
    far.finish((grad_weight, next_sum.terms))
    next_sum.second()
    last = shifted(nz - 3, far.terms[rows:], "sum_3_z")
    onward = shifted(nz - 1, far.terms[:rows], "sum_2_z")
    ask = tie(hidden_table, own_sum.sent, next_sum.sent, far.terms)
    grad_hidden = hidden_gradient(
        gate[count:],
        slot_of[count:],
        grads_2 + others_2,
        weight,
        ask,
        capacity,
        back,
    )
    own_sum.finish(grad_hidden)
    own_sum.second()
    next_sum.finish(grad_hidden)
    onward, last = tie((onward, last), grad_hidden)
    onward = tie(onward, last) + next_sum.terms
    onward = shifted(nz - 1, onward, "sum_1_z")
    own_sum.finish(grad_hidden)
    mixed_out = own_sum.terms.astype(F32) + last.astype(F32) + onward.astype(F32)
    return (mixed_out.astype(BF16), grad_hidden[None], grad_weight[None])


def solution(mesh):
    return jax.shard_map(
        body,
        mesh=mesh,
        in_specs=(
            P("expert", None, "dp"),
            P("expert", "dp", None),
            P("dp", "expert"),
            P("dp", None),
            P("dp", None),
        ),
        out_specs=(P("dp", "expert"), P("expert", None, "dp"), P("expert", "dp", None)),
        check_vma=False,
    )
```
